256 devices in a mesh: src: 32 (over y, z_hi, x), freq: 8 (over z_lo, core).
Axes of the slice: x: 4, y: 4, z: 8 (z_hi: 2, z_lo: 4; z = z_hi * 4 + z_lo), core: 2. Of those that a mesh axis runs over, the one named last changes fastest.
Arguments:
- source_dirs: float32 [2, 16384], P(None, 'src'), may hold values from -0.6 to 0.6
- flux: float32 [16384], P('src'), may hold values from 0.1 to 10
- beam: float32 [256, 16384], P('freq', 'src'), may hold values from 0.3 to 1
- counts: int32 [32], replicated, may hold values from 1 to 512, 8192 in all
- antennas: float32 [3, 128], replicated, may hold values from -30 to 30
- pairs: int32 [2, 4096], replicated, may hold values from 0 to 127, as said below
- data: float32 [2, 256, 4096], P(None, None, ('src', 'freq')), may hold values from -6 to 6
- delay_weight: float32 [256], replicated, may hold values from 0.3 to 3
Outputs:
- flux_grad: float32 [16384], P('src')
- beam_grad: float32 [256, 16384], P('freq', 'src')
The draws below stay inside these ranges and needn't reach their ends.
Inputs may be any that keep to these rules, and one draw needn't show every extreme that they name: Live sources fill the first slots of each block; the counts sum to 8192 and the largest is exactly 512. `pairs`: each baseline names two different antennas.
All inputs are finite; a program needn't handle non-finite values.
Results may differ from the reference program's by a relative error of at most 0.0003.
Values sent between devices are 32-bit elements; how exact they have to be, the bound alone decides.
A program may use at most 128 MiB of HBM per device.

```python
import math
import jax
import jax.numpy as jnp
import numpy as np
from jax import lax

ANTENNA_COUNT = 128
NCH = 256
BASELINE_COUNT = 4096
SRC_DEV = 512
NSRC = 16384
N_SRC = 32


def draw_pairs(key, part):
    key = jax.random.fold_in(key, 7)
    random_key_start, random_key_stride = jax.random.split(key)
    antenna_left = jax.random.randint(random_key_start, (BASELINE_COUNT,), 0, ANTENNA_COUNT)
    antenna_stride = jax.random.randint(random_key_stride, (BASELINE_COUNT,), 1, ANTENNA_COUNT)
    antenna_right = (antenna_left + antenna_stride) % ANTENNA_COUNT
    return jnp.stack([antenna_left, antenna_right]).astype(jnp.int32)


def block_levels(stream_key, extent, cuts, least, largest):
    def one(position, blocks):
        steps = jax.random.uniform(jax.random.fold_in(jax.random.fold_in(stream_key, 6), position), (blocks,), jnp.float32, least / len(cuts), largest / len(cuts))
        return jnp.repeat(jnp.exp(steps), extent[position] // blocks).reshape((-1,) + (1,) * (len(extent) - position - 1))

    loudness = one(*cuts[0])
    for cut in cuts[1:]:
        loudness = loudness * one(*cut)
    return loudness


def length_profile(number_of, total, limit, slope):
    loads = [(1 << 20) // math.isqrt(rank ** slope) + 1 for rank in range(2, number_of + 1)]
    surplus, holding = total - limit - (number_of - 1), [1] * (number_of - 1)
    while surplus > 0:
        free = [i for i in range(number_of - 1) if holding[i] < limit]
        mass, remaining = sum([loads[i] for i in free]), surplus
        for i in free:
            addition = min(limit - holding[i], max(1, remaining * loads[i] // mass), surplus)
            holding[i] = holding[i] + addition
            surplus = surplus - addition
    return np.array([limit] + holding)


def ragged_sizes(own_key, count, total, reach, skew):
    if count == 2:
        one = jax.random.randint(own_key, (), max(1, total - reach), min(reach, total - 1) + 1)
        return jnp.stack([one, total - one])
    tallies = jnp.asarray(length_profile(count, total, reach, skew), jnp.int32)
    twos = (count - 1) // 2
    source_of, receiver = tallies[1:1 + 2 * twos:2], tallies[2:2 + 2 * twos:2]
    room = jnp.minimum(source_of - 1, reach - receiver)
    passed = jax.random.randint(jax.random.fold_in(own_key, 1), (twos,), 0, 1 << 20) % (room + 1)
    tallies = tallies.at[1:1 + 2 * twos:2].set(source_of - passed).at[2:2 + 2 * twos:2].set(receiver + passed)
    return tallies[jax.random.permutation(jax.random.fold_in(own_key, 2), count)]


def scatter_about(own_key, extent, width, most, cuts=(), kind=jnp.bfloat16):
    gain = block_levels(own_key, extent, cuts, -0.22, 0.18) if cuts else 1.0
    values = jax.random.normal(own_key, extent, jnp.float32) * width * gain
    return jnp.minimum(jnp.maximum(values, -most), most).astype(kind)


def setup_inputs(seed: int = 0) -> dict:
    arg_keys = jax.random.split(jax.random.key(seed), 9)
    return {
        "source_dirs": jnp.clip(jax.random.uniform(arg_keys[0], (2, NSRC), jnp.float32, -0.6, 0.6) * block_levels(arg_keys[0], (2, NSRC), ((1, 32),), -0.4, 0.0), -0.6, 0.6),
        "flux": jnp.clip(jnp.exp(math.log(10.0) - 4.6051702 * jax.random.uniform(arg_keys[1], (NSRC,), jnp.float32) ** block_levels(arg_keys[1], (NSRC,), ((0, 32),), -0.2, 0.2)), 0.1, 10.0),
        "beam": jnp.clip(0.3 + 0.7 * jax.random.uniform(arg_keys[2], (NCH, NSRC), jnp.float32) ** block_levels(arg_keys[2], (NCH, NSRC), ((0, 8), (1, 32)), -0.2, 0.2), 0.3, 1.0),
        "counts": ragged_sizes(arg_keys[3], N_SRC, NSRC // 2, SRC_DEV, 2).astype(jnp.int32),
        "antennas": jnp.clip(jax.random.uniform(arg_keys[4], (3, ANTENNA_COUNT), jnp.float32, -30.0, 30.0), -30.0, 30.0),
        "pairs": draw_pairs(jax.random.fold_in(arg_keys[8], 71), 0),
        "data": scatter_about(arg_keys[6], (2, NCH, BASELINE_COUNT), 1.0, 6.0, ((2, 256),), jnp.float32),
        "delay_weight": jnp.clip(jnp.exp(jax.random.uniform(arg_keys[7], (NCH,), jnp.float32, math.log(0.3), math.log(3.0))), 0.3, 3.0),
    }


TWO_PI = 2.0 * math.pi
PRECISE = lax.Precision.HIGHEST

def precise_dot(left, right):
    return jnp.dot(left, right, precision=PRECISE, preferred_element_type=jnp.float32)

def channel_freqs(chan_index):
    return 1.0 + 0.6 * chan_index.astype(jnp.float32) / NCH

def phase_matrix(dir_block, antennas, chan_freqs):
    along_l = dir_block[0]
    along_m = dir_block[1]
    along_n = jnp.sqrt(1.0 - along_l * along_l - along_m * along_m)
    delay = antennas[0][:, None] * along_l[None, :] + antennas[1][:, None] * along_m[None, :] + antennas[2][:, None] * along_n[None, :]
    phase = (TWO_PI * chan_freqs)[:, None, None] * delay[None, :, :]
    return jnp.concatenate([jnp.cos(phase), jnp.sin(phase)], axis=1)

def gram_of(phased, weights):
    return jnp.einsum('cas,cbs->cab', phased * weights[:, None, :], phased, precision=PRECISE, preferred_element_type=jnp.float32)

def baseline_values(inner_product_matrix, pairs):
    antenna_left = pairs[0]
    antenna_right = pairs[1]
    antenna_total = inner_product_matrix.shape[1] // 2
    real_component = inner_product_matrix[:, antenna_left, antenna_right] + inner_product_matrix[:, antenna_left + antenna_total, antenna_right + antenna_total]
    imaginary_component = inner_product_matrix[:, antenna_left + antenna_total, antenna_right] - inner_product_matrix[:, antenna_left, antenna_right + antenna_total]
    return jnp.stack([real_component, imaginary_component])

def delay_tables():
    chan_index = jnp.arange(NCH, dtype=jnp.int32)
    turn_count = chan_index[:, None] * chan_index[None, :] % NCH
    angles = TWO_PI * turn_count.astype(jnp.float32) / NCH
    table_scale = 1.0 / math.sqrt(NCH)
    window_taper = 0.6 - 0.4 * jnp.cos(TWO_PI * (chan_index.astype(jnp.float32) + 0.5) / NCH)
    return (jnp.cos(angles) * table_scale, -jnp.sin(angles) * table_scale, window_taper)

def spectral_cotangent(visibility, data, delay_weight):
    cos_table, sin_table, window_taper = delay_tables()
    tapered_re = window_taper[:, None] * visibility[0]
    tapered_im = window_taper[:, None] * visibility[1]
    spec_re = precise_dot(cos_table, tapered_re) - precise_dot(sin_table, tapered_im)
    spec_im = precise_dot(cos_table, tapered_im) + precise_dot(sin_table, tapered_re)
    grad_re = delay_weight[:, None] * (spec_re - data[0])
    grad_im = delay_weight[:, None] * (spec_im - data[1])
    back_re = precise_dot(cos_table.T, grad_re) + precise_dot(sin_table.T, grad_im)
    back_im = precise_dot(cos_table.T, grad_im) - precise_dot(sin_table.T, grad_re)
    return jnp.stack([window_taper[:, None] * back_re, window_taper[:, None] * back_im])

def transpose_solver(upstream_gradient, pairs, antenna_total):
    channel_total = upstream_gradient.shape[1]
    blank_canvas = jnp.zeros((channel_total, antenna_total, antenna_total), jnp.float32)
    cot_real = blank_canvas.at[:, pairs[0], pairs[1]].add(upstream_gradient[0])
    cot_imag = blank_canvas.at[:, pairs[0], pairs[1]].add(upstream_gradient[1])
    upper_rows = jnp.concatenate([cot_real, -cot_imag], axis=2)
    lower_rows = jnp.concatenate([cot_imag, cot_real], axis=2)
    return jnp.concatenate([upper_rows, lower_rows], axis=1)

def weight_grads(kernel, phased):
    product = jnp.einsum('cab,cbs->cas', kernel, phased, precision=PRECISE, preferred_element_type=jnp.float32)
    return lax.optimization_barrier(jnp.sum(phased * product, axis=1))

def reference(source_dirs, flux, beam, counts, antennas, pairs, data, delay_weight):
    chan_freqs = channel_freqs(jnp.arange(NCH, dtype=jnp.int32))
    slot_index = jnp.arange(SRC_DEV, dtype=jnp.int32)
    live_mask = (slot_index[None, :] < counts[:, None]).astype(jnp.float32).reshape(NSRC)
    live_scale = live_mask * (1.0 / math.sqrt(NSRC))
    weights = flux[None, :] * beam * beam * live_scale[None, :]
    block_ids = jnp.arange(N_SRC, dtype=jnp.int32)

    def forward_step(running_sum, block_id):
        block_start = (block_id * SRC_DEV).astype(jnp.int32)
        dir_block = lax.dynamic_slice_in_dim(source_dirs, block_start, SRC_DEV, 1)
        weight_block = lax.dynamic_slice_in_dim(weights, block_start, SRC_DEV, 1)
        phased = phase_matrix(dir_block, antennas, chan_freqs)
        return (running_sum + gram_of(phased, weight_block), jnp.zeros((), jnp.float32))
    gram_total = lax.scan(forward_step, jnp.zeros((NCH, 2 * ANTENNA_COUNT, 2 * ANTENNA_COUNT), jnp.float32), block_ids)[0]
    visibility = baseline_values(gram_total, pairs)
    upstream_gradient = spectral_cotangent(visibility, data, delay_weight)
    kernel = transpose_solver(upstream_gradient, pairs, ANTENNA_COUNT)

    def backward_step(carried, block_id):
        block_start = (block_id * SRC_DEV).astype(jnp.int32)
        dir_block = lax.dynamic_slice_in_dim(source_dirs, block_start, SRC_DEV, 1)
        phased = phase_matrix(dir_block, antennas, chan_freqs)
        return (carried, weight_grads(kernel, phased))
    stacked = lax.scan(backward_step, jnp.zeros((), jnp.float32), block_ids)[1]
    all_grads = jnp.transpose(stacked, (1, 0, 2)).reshape(NCH, NSRC)
    flux_grad = lax.optimization_barrier(jnp.sum(all_grads * beam * beam, axis=0)) * live_scale
    beam_grad = all_grads * (2.0 * flux * live_scale)[None, :] * beam
    return (flux_grad, beam_grad)
```

```python
import functools
import math

import jax
import jax.numpy as jnp
import numpy as np
from jax import lax
from jax.experimental import pallas as pl
from jax.experimental.pallas import tpu as pltpu
from jax.sharding import PartitionSpec as P

TWO_PI = 2.0 * math.pi
MESH = pl.DeviceIdType.MESH
F32 = jnp.float32
BF16 = jnp.bfloat16
LANES = 128
NT = (((1,), (1,)), ((), ()))
NN = (((1,), (0,)), ((), ()))
SIN_POLY = (6.283184916495431, -41.34158923268848, 81.59994332978007, -76.61447253122434, 41.34288235446963, -12.471243534886277)
COS_POLY = (0.9999999890590217, -19.73920449945381, 64.93911745989173, -85.45013953082399, 60.16763095051855, -25.967599246994247, 6.528658159389057)


def dot(left, right, dims=NN):
    return lax.dot_general(left, right, dims, preferred_element_type=F32)


def split(value):
    high = value.astype(BF16)
    return high, (value - high.astype(F32)).astype(BF16)


def horner(coefficients, variable):
    total = coefficients[-1] * variable + coefficients[-2]
    for coefficient in coefficients[-3::-1]:
        total = total * variable + coefficient
    return total


def sin_cos_turns(turns):
    rest = turns - jnp.round(turns)
    square = rest * rest
    return rest * horner(SIN_POLY, square), horner(COS_POLY, square)


def delay_tables(nch):
    index = np.arange(nch)
    angle = 2.0 * np.pi * ((index[:, None] * index[None, :]) % nch) / nch
    taper = 0.6 - 0.4 * np.cos(2.0 * np.pi * (index + 0.5) / nch)
    cos, sin = np.cos(angle) / math.sqrt(nch), np.sin(angle) / math.sqrt(nch)
    forward = np.zeros((2, nch, nch, 2))
    forward[0, :, :, 0] = cos
    forward[0, :, :, 1] = sin
    forward[1, :, :, 0] = -sin
    forward[1, :, :, 1] = cos
    forward *= taper[None, None, :, None]
    forward = forward.reshape(2 * nch, 2 * nch)
    return np.stack([forward, forward.T]).astype(np.float32)


def peer_at(own, step, count):
    if count != 32:
        return lax.rem(own + step, count)
    own_x, own_z, own_y = lax.rem(own, 4), lax.rem(own // 4, 2), own // 8
    x = lax.rem(own_x + lax.rem(step, 4), 4)
    y = lax.rem(own_y + lax.rem(step // 4, 4), 4)
    z = lax.rem(own_z + step // 16, 2)
    return y * 8 + z * 4 + x


def kernel(
    ns, nf, centre,
    dirs_ref, flux_ref, beam_ref, counts_ref, ant_ref, pairs_ref, data_ref, dw_ref, tables_hbm,
    u_ref, total_ref,
    source_send, source_recv, phased_hi, phased_lo, one_left, one_right, ant_cols, gram_ref,
    vis_send, vis_recv, vis_rows, vis_all, dat_recv, tables, cot_all, cot_rows, cot_send, cot_recv,
    u_send, u_recv, flux_send, flux_recv,
    table_sem, send1, recv1, send2, recv2, send3, recv3, send4, recv4, send5, recv5, send6, recv6, send7, recv7,
    send8, recv8,
):
    nch = ns * nf
    slots = dirs_ref.shape[1]
    nb = ns * LANES
    rows = 2 * ns
    s = lax.axis_index("src")
    q = lax.axis_index("freq")

    barrier = pltpu.get_barrier_semaphore()

    def greet_src(step, carry):
        pl.semaphore_signal(barrier, inc=1, device_id={"src": peer_at(s, step, ns)}, device_id_type=MESH)
        return carry

    def greet_freq(step, carry):
        pl.semaphore_signal(barrier, inc=1, device_id={"freq": lax.rem(q + step, nf)}, device_id_type=MESH)
        return carry

    lax.fori_loop(1, ns, greet_src, 0)
    lax.fori_loop(1, nf, greet_freq, 0)
    table_copy = pltpu.make_async_copy(tables_hbm, tables, table_sem)
    table_copy.start()

    along_l, along_m = dirs_ref[0:1, :], dirs_ref[1:2, :]
    along_n = jnp.sqrt(1.0 - along_l * along_l - along_m * along_m)
    live = lax.broadcasted_iota(jnp.int32, (1, slots), 1) < counts_ref[s]
    strength = jnp.where(live, jnp.sqrt(flux_ref[...] * (1.0 / math.sqrt(slots * ns))), 0.0)
    roots = beam_ref[...] * strength
    for i in range(ns):
        source_send[i, 0:1, :] = along_l
        source_send[i, 1:2, :] = along_m
        source_send[i, 2:3, :] = along_n
        source_send[i, 3:4, :] = roots[i : i + 1, :]
    source_recv[s] = source_send[s]

    pl.semaphore_wait(barrier, ns - 1 + nf - 1)

    def send_sources(step, carry):
        peer = peer_at(s, ns - step, ns)
        pltpu.make_async_remote_copy(
            src_ref=source_send.at[peer], dst_ref=source_recv.at[s], send_sem=send1, recv_sem=recv1.at[s],
            device_id={"src": peer}, device_id_type=MESH,
        ).start()
        return carry

    lax.fori_loop(1, ns, send_sources, 0)

    @pl.when(q == centre)
    def _():
        dat_recv[q] = data_ref[...]

    @pl.when(q != centre)
    def _():
        pltpu.make_async_remote_copy(
            src_ref=data_ref, dst_ref=dat_recv.at[q], send_sem=send2, recv_sem=recv2.at[q],
            device_id={"freq": centre}, device_id_type=MESH,
        ).start()

    freq = 1.0 + 0.6 * (q * ns + s).astype(F32) / nch
    for i in range(3):
        ant_cols[i] = jnp.transpose(jnp.broadcast_to(ant_ref[i : i + 1, :] * freq, (LANES, LANES)))

    antenna_id = lax.broadcasted_iota(jnp.int32, (LANES, 512), 0)

    def build_one_hot(j, carry):
        at = pl.ds(pl.multiple_of(j * 512, 512), 512)
        one_left[:, at] = (antenna_id == pairs_ref[0:1, at]).astype(F32).astype(BF16)
        one_right[:, at] = (antenna_id == pairs_ref[1:2, at]).astype(F32).astype(BF16)
        return carry

    lax.fori_loop(0, nb // 512, build_one_hot, 0)

    gram_ref[...] = jnp.zeros_like(gram_ref)

    def forward(step, carry):
        k = peer_at(s, step, ns)

        @pl.when(step > 0)
        def _():
            pltpu.make_async_remote_copy(
                src_ref=source_send.at[k], dst_ref=source_recv.at[k], send_sem=send1, recv_sem=recv1.at[k],
                device_id={"src": k}, device_id_type=MESH,
            ).wait_recv()

        for lane in range(0, slots, LANES):
            at = pl.ds(lane, LANES)
            row_l, row_m = source_recv[k, 0:1, at], source_recv[k, 1:2, at]
            row_n, root = source_recv[k, 2:3, at], source_recv[k, 3:4, at]
            for first in range(0, LANES, 64):
                ants = pl.ds(first, 64)
                turns = ant_cols[0, ants, :] * row_l + ant_cols[1, ants, :] * row_m + ant_cols[2, ants, :] * row_n
                sine, cosine = sin_cos_turns(turns)
                for base, value in ((0, cosine * root), (LANES, sine * root)):
                    high = value.astype(BF16)
                    phased_hi[k, pl.ds(base + first, 64), at] = high
                    phased_lo[k, pl.ds(base + first, 64), at] = (2.0 * (value - high.astype(F32))).astype(BF16)
        high = phased_hi[k]
        gram_ref[...] += dot(high, high, NT) + dot(high, phased_lo[k], NT)
        return carry

    lax.fori_loop(0, ns, forward, 0)

    gram = gram_ref[...]
    even = gram[:LANES, :LANES] + gram[LANES:, LANES:]
    odd = gram[LANES:, :LANES] - gram[:LANES, LANES:]
    vis_re = 0.5 * (even + even.T)
    vis_im = 0.5 * (odd - odd.T)
    grid_hi, grid_lo = split(jnp.concatenate([vis_re, -vis_im], axis=0))

    def gather(j, carry):
        at = pl.ds(pl.multiple_of(j * 512, 512), 512)
        left = one_left[:, at]
        picked = dot(grid_hi, left) + dot(grid_lo, left)
        right = one_right[:, at].astype(F32)
        real = jnp.sum(picked[:LANES] * right, axis=0, keepdims=True)
        imag = jnp.sum(picked[LANES:] * right, axis=0, keepdims=True)
        for i in range(4):
            vis_send[j * 4 + i, 0:1, :] = real[:, i * LANES : (i + 1) * LANES]
            vis_send[j * 4 + i, 1:2, :] = imag[:, i * LANES : (i + 1) * LANES]
        return carry

    lax.fori_loop(0, nb // 512, gather, 0)

    def send_vis(step, carry):
        peer = peer_at(s, ns - step, ns)
        pltpu.make_async_remote_copy(
            src_ref=vis_send.at[peer], dst_ref=vis_recv.at[s], send_sem=send3, recv_sem=recv3,
            device_id={"src": peer}, device_id_type=MESH,
        ).start()
        return carry

    lax.fori_loop(1, ns, send_vis, 0)
    vis_recv[s] = vis_send[s]
    most = pl.ds(0, ns - 1)
    pltpu.make_async_copy(vis_send.at[most], vis_recv.at[most], recv3).wait()
    for i in range(ns):
        vis_rows[2 * i : 2 * i + 2, :] = vis_recv[i]

    @pl.when(q != centre)
    def _():
        pltpu.make_async_remote_copy(
            src_ref=vis_rows, dst_ref=vis_all.at[q], send_sem=send4, recv_sem=recv4.at[q],
            device_id={"freq": centre}, device_id_type=MESH,
        ).start()

    table_copy.wait()

    @pl.when(q == centre)
    def _():
        vis_all[q] = vis_rows[...]

        def take_data(step, carry):
            other = lax.rem(q + step, nf)
            pltpu.make_async_remote_copy(
                src_ref=data_ref, dst_ref=dat_recv.at[other], send_sem=send2, recv_sem=recv2.at[other],
                device_id={"freq": other}, device_id_type=MESH,
            ).wait_recv()
            return carry

        lax.fori_loop(1, nf, take_data, 0)
        weight = jnp.transpose(jnp.broadcast_to(dw_ref[...], (LANES, nch)))
        spectra = [
            jnp.transpose(jnp.concatenate([dat_recv[i, c] for i in range(nf)], axis=0)) for c in range(2)
        ]

        there_hi, there_lo = split(tables[0])
        back_hi, back_lo = split(tables[1])

        def take_vis(step, carry):
            other = lax.rem(q + step, nf)
            pltpu.make_async_remote_copy(
                src_ref=vis_rows, dst_ref=vis_all.at[other], send_sem=send4, recv_sem=recv4.at[other],
                device_id={"freq": other}, device_id_type=MESH,
            ).wait_recv()
            return carry

        lax.fori_loop(1, nf, take_vis, 0)
        vis_hi, vis_lo = split(jnp.concatenate([vis_all[i] for i in range(nf)], axis=0))
        spec = dot(there_hi, vis_hi) + dot(there_hi, vis_lo) + dot(there_lo, vis_hi)
        spec_cot = jnp.concatenate(
            [weight * (spec[:nch] - spectra[0]), weight * (spec[nch:] - spectra[1])], axis=0
        )
        cot_hi, cot_lo = split(spec_cot)
        back = dot(back_hi, cot_hi) + dot(back_hi, cot_lo) + dot(back_lo, cot_hi)
        for i in range(nf):
            cot_all[i] = back[i * rows : (i + 1) * rows]

        def send_cot(step, carry):
            other = lax.rem(q + step, nf)
            pltpu.make_async_remote_copy(
                src_ref=cot_all.at[other], dst_ref=cot_rows, send_sem=send5, recv_sem=recv5,
                device_id={"freq": other}, device_id_type=MESH,
            ).start()
            return carry

        lax.fori_loop(1, nf, send_cot, 0)
        cot_rows[...] = cot_all[q]

    @pl.when(q != centre)
    def _():
        pltpu.make_async_remote_copy(
            src_ref=cot_all.at[q], dst_ref=cot_rows, send_sem=send5, recv_sem=recv5,
            device_id={"freq": centre}, device_id_type=MESH,
        ).wait_recv()

    for i in range(ns):
        cot_send[i] = cot_rows[2 * i : 2 * i + 2, :]

    def fan_out(step, carry):
        peer = peer_at(s, ns - step, ns)
        pltpu.make_async_remote_copy(
            src_ref=cot_send.at[peer], dst_ref=cot_recv.at[s], send_sem=send6, recv_sem=recv6,
            device_id={"src": peer}, device_id_type=MESH,
        ).start()
        return carry

    lax.fori_loop(1, ns, fan_out, 0)
    cot_recv[s] = cot_send[s]
    pltpu.make_async_copy(cot_send.at[most], cot_recv.at[most], recv6).wait()

    def scatter(j, total):
        at = pl.ds(pl.multiple_of(j * 512, 512), 512)
        right = one_right[:, at]
        parts = []
        for c in range(2):
            row = jnp.concatenate([cot_recv[j * 4 + i, c : c + 1, :] for i in range(4)], axis=1)
            parts.append(split(row))
        scaled = [right * parts[c][part] for part in range(2) for c in range(2)]
        return total + dot(one_left[:, at], jnp.concatenate(scaled, axis=0), NT)

    grids = lax.fori_loop(0, nb // 512, scatter, jnp.zeros((LANES, 4 * LANES), F32))
    grids = grids[:, : 2 * LANES] + grids[:, 2 * LANES :]
    real, imag = grids[:, :LANES], grids[:, LANES:]
    real, imag = 0.5 * (real + real.T), 0.5 * (imag - imag.T)
    matrix = jnp.concatenate(
        [jnp.concatenate([real, -imag], axis=1), jnp.concatenate([imag, real], axis=1)], axis=0
    )
    matrix_hi, matrix_lo = split(matrix)
    gram_ref[...] = matrix

    def backward(step, carry):
        k = peer_at(s, ns - step, ns)
        high = phased_hi[k]
        product = dot(matrix_hi, high) + dot(matrix_lo, high)
        phased = high.astype(F32) + phased_lo[k].astype(F32)
        u_send[k] = jnp.sum(phased * product, axis=0, keepdims=True)

        @pl.when(step < ns)
        def _():
            pltpu.make_async_remote_copy(
                src_ref=u_send.at[k], dst_ref=u_recv.at[s], send_sem=send7, recv_sem=recv7,
                device_id={"src": k}, device_id_type=MESH,
            ).start()

        return carry

    lax.fori_loop(1, ns + 1, backward, 0)
    u_recv[s] = u_send[s]
    pltpu.make_async_copy(u_send.at[most], u_recv.at[most], recv7).wait()
    for i in range(ns):
        u_ref[i : i + 1, :] = u_recv[i]
    flux_send[0] = jnp.sum(u_ref[...], axis=0, keepdims=True)

    def send_flux(step, carry):
        other = lax.rem(q + step, nf)
        pltpu.make_async_remote_copy(
            src_ref=flux_send, dst_ref=flux_recv.at[pl.ds(q, 1)], send_sem=send8, recv_sem=recv8,
            device_id={"freq": other}, device_id_type=MESH,
        ).start()
        return carry

    lax.fori_loop(1, nf, send_flux, 0)
    flux_recv[q] = flux_send[0]
    others = pl.ds(0, nf - 1)
    pltpu.make_async_copy(flux_recv.at[others], flux_recv.at[others], recv8).wait()
    total = flux_recv[0]
    for i in range(1, nf):
        total = total + flux_recv[i]
    total_ref[...] = total

    pltpu.make_async_copy(source_send.at[most], source_recv.at[most], send1).wait()
    pltpu.make_async_copy(vis_send.at[most], vis_recv.at[most], send3).wait()
    pltpu.make_async_copy(cot_send.at[most], cot_recv.at[most], send6).wait()
    pltpu.make_async_copy(u_send.at[most], u_recv.at[most], send7).wait()
    pltpu.make_async_copy(flux_recv.at[others], flux_recv.at[others], send8).wait()

    @pl.when(q == centre)
    def _():
        pltpu.make_async_copy(cot_all.at[others], cot_all.at[others], send5).wait()

    @pl.when(q != centre)
    def _():
        pltpu.make_async_copy(data_ref, dat_recv.at[0], send2).wait()
        pltpu.make_async_copy(vis_rows, vis_rows, send4).wait()


def body(source_dirs, flux, beam, counts, antennas, pairs, data, delay_weight):
    ns, nf = lax.axis_size("src"), lax.axis_size("freq")
    slots = flux.shape[0]
    nch = ns * nf
    share = LANES // nf
    rows = 2 * ns
    vmem, smem = pl.BlockSpec(memory_space=pltpu.VMEM), pl.BlockSpec(memory_space=pltpu.SMEM)
    dma = pltpu.SemaphoreType.DMA
    macs = 4 * ns * slots * 256 * 256
    gradient, total = pl.pallas_call(
        functools.partial(kernel, ns, nf, min(3, nf - 1)),
        out_shape=(
            jax.ShapeDtypeStruct((ns, slots), F32),
            jax.ShapeDtypeStruct((1, slots), F32),
        ),
        in_specs=[vmem, vmem, vmem, smem, vmem, vmem, vmem, vmem, pl.BlockSpec(memory_space=pltpu.HBM)],
        out_specs=(vmem, vmem),
        scratch_shapes=[
            pltpu.VMEM((ns, 4, slots), F32),
            pltpu.VMEM((ns, 4, slots), F32),
            pltpu.VMEM((ns, 2 * LANES, slots), BF16),
            pltpu.VMEM((ns, 2 * LANES, slots), BF16),
            pltpu.VMEM((LANES, ns * LANES), BF16),
            pltpu.VMEM((LANES, ns * LANES), BF16),
            pltpu.VMEM((3, LANES, LANES), F32),
            pltpu.VMEM((2 * LANES, 2 * LANES), F32),
            pltpu.VMEM((ns, 2, LANES), F32),
            pltpu.VMEM((ns, 2, LANES), F32),
            pltpu.VMEM((rows, LANES), F32),
            pltpu.VMEM((nf, rows, LANES), F32),
            pltpu.VMEM((nf, 2, share, nch), F32),
            pltpu.VMEM((2, 2 * nch, 2 * nch), F32),
            pltpu.VMEM((nf, rows, LANES), F32),
            pltpu.VMEM((rows, LANES), F32),
            pltpu.VMEM((ns, 2, LANES), F32),
            pltpu.VMEM((ns, 2, LANES), F32),
            pltpu.VMEM((ns, 1, slots), F32),
            pltpu.VMEM((ns, 1, slots), F32),
            pltpu.VMEM((1, 1, slots), F32),
            pltpu.VMEM((nf, 1, slots), F32),
            dma,
            dma, dma((ns,)),
            dma, dma((nf,)),
            dma, dma,
            dma, dma((nf,)),
            dma, dma,
            dma, dma,
            dma, dma,
            dma, dma,
        ],
        compiler_params=pltpu.CompilerParams(
            collective_id=0, has_side_effects=True, vmem_limit_bytes=48 * 1024 * 1024
        ),
        cost_estimate=pl.CostEstimate(flops=2 * macs, bytes_accessed=4 * 1024 * 1024, transcendentals=0),
    )(
        source_dirs, flux[None, :], beam, counts, antennas, pairs, jnp.transpose(data, (0, 2, 1)), delay_weight[None, :],
        jnp.asarray(delay_tables(nch)),
    )
    return (total[0] / flux, 2.0 * gradient / beam)


def solution(mesh):
    in_specs = (
        P(None, "src"),
        P("src"),
        P("freq", "src"),
        P(),
        P(),
        P(),
        P(None, None, ("src", "freq")),
        P(),
    )
    out_specs = (P("src"), P("freq", "src"))
    return jax.shard_map(body, mesh=mesh, in_specs=in_specs, out_specs=out_specs, check_vma=False)
```

```python
import functools
import math

import jax
import jax.numpy as jnp
import numpy as np
from jax import lax
from jax.experimental import pallas as pl
from jax.experimental.pallas import tpu as pltpu
from jax.sharding import PartitionSpec as P

TWO_PI = 2.0 * math.pi
MESH = pl.DeviceIdType.MESH
F32 = jnp.float32
BF16 = jnp.bfloat16
LANES = 128
NT = (((1,), (1,)), ((), ()))
NN = (((1,), (0,)), ((), ()))
SIN_POLY = (3.141592640130707, -5.167710083507862, 2.550077523214134, -0.5982912856178576, 0.0776576603009221)
COS_POLY = (0.9999999532476082, -4.93479283061961, 4.058411352862035, -1.3318765680776314, 0.2196896110917421)


def dot(left, right, dims=NN):
    return lax.dot_general(left, right, dims, preferred_element_type=F32)


def split(value):
    high = value.astype(BF16)
    return high, (value - high.astype(F32)).astype(BF16)


def horner(coefficients, variable):
    total = coefficients[-1] * variable + coefficients[-2]
    for coefficient in coefficients[-3::-1]:
        total = total * variable + coefficient
    return total


def scaled_cos_sin(turns, root):
    rest = turns - jnp.round(turns)
    square = rest * rest
    sine = rest * horner(SIN_POLY, square)
    twice = (2.0 * root) * sine
    return root - twice * sine, twice * horner(COS_POLY, square)


def three_parts(value):
    first = value.astype(BF16).astype(F32)
    rest = value - first
    second = rest.astype(BF16).astype(F32)
    return first, second, (rest - second).astype(BF16).astype(F32)


def delay_tables(nch):
    index = np.arange(nch)
    angle = 2.0 * np.pi * ((index[:, None] * index[None, :]) % nch) / nch
    taper = 0.6 - 0.4 * np.cos(2.0 * np.pi * (index + 0.5) / nch)
    cos, sin = np.cos(angle) / math.sqrt(nch), np.sin(angle) / math.sqrt(nch)
    forward = np.zeros((2, nch, nch, 2))
    forward[0, :, :, 0] = cos
    forward[0, :, :, 1] = sin
    forward[1, :, :, 0] = -sin
    forward[1, :, :, 1] = cos
    forward *= taper[None, None, :, None]
    forward = forward.reshape(2 * nch, 2 * nch)
    return np.stack([forward, forward.T]).astype(np.float32)


def peer_at(own, step, count):
    if count != 32:
        return lax.rem(own + step, count)
    own_x, own_z, own_y = lax.rem(own, 4), lax.rem(own // 4, 2), own // 8
    x = lax.rem(own_x + lax.rem(step, 4), 4)
    y = lax.rem(own_y + lax.rem(step // 4, 4), 4)
    z = lax.rem(own_z + step // 16, 2)
    return y * 8 + z * 4 + x


def quad_at(own, step, count):
    if count != 8:
        return lax.rem(own + step, count)
    y = lax.rem(own // 2 + lax.rem(step, 4), 4)
    z = lax.rem(lax.rem(own, 2) + step // 4, 2)
    return y * 2 + z


def kernel(
    ns, nf, centre,
    dirs_hbm, flux_hbm, beam_hbm, counts_hbm, ant_hbm, pairs_hbm, data_hbm, dw_hbm, tables_hbm,
    u_ref, total_ref,
    dirs_ref, flux_ref, beam_ref, counts_ref, ant_ref, pairs_ref, data_ref, dw_ref, tables,
    source_send, source_recv, phased_hi, phased_lo, left_twice, one_right, ant_parts, even_hi, even_lo, odd_hi, odd_lo, gram_hh, gram_hl,
    vis_send, vis_recv, vis_rows, vis_all, dat_recv, tables_hi, tables_lo, cot_all, cot_rows, cot_send, cot_recv,
    u_send, u_recv, flux_send, flux_recv,
    input_sem, send1, recv1, send2, recv2, send3, recv3, send4, recv4, send5, recv5, send6, recv6, send7, recv7,
    send8, recv8,
):
    nch = ns * nf
    slots = dirs_ref.shape[1]
    nb = ns * LANES
    rows = 2 * ns
    s = lax.axis_index("src")
    q = lax.axis_index("freq")

    inputs = [
        pltpu.make_async_copy(hbm, vmem, input_sem.at[i])
        for i, (hbm, vmem) in enumerate((
            (dirs_hbm, dirs_ref), (flux_hbm, flux_ref), (beam_hbm, beam_ref), (counts_hbm, counts_ref),
            (ant_hbm, ant_ref), (pairs_hbm, pairs_ref), (data_hbm, data_ref), (dw_hbm, dw_ref),
            (tables_hbm, tables),
        ))
    ]
    for copy in inputs:
        copy.start()
    barrier = pltpu.get_barrier_semaphore()

    def greet_src(step, carry):
        pl.semaphore_signal(barrier, inc=1, device_id={"src": peer_at(s, ns - step, ns)}, device_id_type=MESH)
        return carry

    def greet_freq(step, carry):
        pl.semaphore_signal(barrier, inc=1, device_id={"freq": lax.rem(q + step, nf)}, device_id_type=MESH)
        return carry

    lax.fori_loop(1, ns, greet_src, 0)
    lax.fori_loop(1, nf, greet_freq, 0)
    for copy in inputs[:8]:
        copy.wait()

    along_l, along_m = dirs_ref[0:1, :], dirs_ref[1:2, :]
    along_n = jnp.sqrt(1.0 - along_l * along_l - along_m * along_m)
    live = lax.broadcasted_iota(jnp.int32, (1, slots), 1) < counts_ref[s]
    strength = jnp.where(live, jnp.sqrt(flux_ref[...] * (1.0 / math.sqrt(slots * ns))), 0.0)
    roots = beam_ref[...] * strength
    for i in range(ns):
        source_send[i, 0:1, :] = along_l
        source_send[i, 1:2, :] = along_m
        source_send[i, 2:3, :] = along_n
        source_send[i, 3:4, :] = roots[i : i + 1, :]
    source_recv[s] = source_send[s]

    freq = 1.0 + 0.6 * (q * ns + s).astype(F32) / nch
    first, second, third = three_parts(
        jnp.concatenate([ant_ref[...] * freq, jnp.zeros((5, LANES), F32)], axis=0)
    )
    spare = jnp.zeros((LANES - 48, LANES), F32)
    ant_parts[...] = jnp.transpose(
        jnp.concatenate([first, second, third, first, second, first, spare], axis=0)
    ).astype(BF16)

    gram_hh[...] = jnp.zeros_like(gram_hh)
    gram_hl[...] = jnp.zeros_like(gram_hl)

    def expand(k, high_ref, low_ref):
        source = jnp.concatenate([source_recv[k], jnp.zeros((4, slots), F32)], axis=0)
        first, second, third = three_parts(source)
        parts = jnp.concatenate([first, first, first, second, second, third], axis=0).astype(BF16)
        turns = dot(ant_parts[:, :48], parts)
        for lane in range(0, slots, LANES):
            root = source_recv[k, 3:4, pl.ds(lane, LANES)]
            for top in range(0, LANES, 64):
                cosine, sine = scaled_cos_sin(turns[top : top + 64, lane : lane + LANES], root)
                for base, value in ((0, cosine), (LANES, sine)):
                    high, low = split(value)
                    at = (pl.ds(base + top, 64), pl.ds(lane, LANES))
                    phased_hi[(k, *at)] = high
                    phased_lo[(k, *at)] = low
                    high_ref[at] = high
                    low_ref[at] = low

    def correlate(high_ref, low_ref):
        high = high_ref[...]
        gram_hh[...] += dot(high, high, NT)
        gram_hl[...] += dot(high, low_ref[...], NT)

    expand(s, even_hi, even_lo)

    antenna_id = lax.broadcasted_iota(jnp.int32, (LANES, 512), 0)

    def build_one_hot(j, carry):
        at = pl.ds(pl.multiple_of(j * 512, 512), 512)
        left = (antenna_id == pairs_ref[0:1, at]).astype(F32).astype(BF16)
        left_twice[:LANES, at] = left
        left_twice[LANES:, at] = left
        one_right[:, at] = (antenna_id == pairs_ref[1:2, at]).astype(F32).astype(BF16)
        return carry

    lax.fori_loop(0, nb // 512, build_one_hot, 0)
    inputs[8].wait()

    @pl.when(q == centre)
    def _():
        piece = min(64, 2 * nch)

        def split_tables(j, carry):
            at = pl.ds(pl.multiple_of(j * piece, piece), piece)
            for i in range(2):
                tables_hi[i, at, :], tables_lo[i, at, :] = split(tables[i, at, :])
            return carry

        lax.fori_loop(0, 2 * nch // piece, split_tables, 0)

    pl.semaphore_wait(barrier, ns - 1 + nf - 1)

    def send_sources(step, carry):
        peer = peer_at(s, ns - step, ns)
        pltpu.make_async_remote_copy(
            src_ref=source_send.at[peer], dst_ref=source_recv.at[s], send_sem=send1, recv_sem=recv1.at[s],
            device_id={"src": peer}, device_id_type=MESH,
        ).start()
        return carry

    lax.fori_loop(1, ns, send_sources, 0)

    @pl.when(q == centre)
    def _():
        dat_recv[q] = data_ref[...]

    @pl.when(q != centre)
    def _():
        pltpu.make_async_remote_copy(
            src_ref=data_ref, dst_ref=dat_recv.at[q], send_sem=send2, recv_sem=recv2.at[q],
            device_id={"freq": centre}, device_id_type=MESH,
        ).start()

    def arrival(step):
        k = peer_at(s, step, ns)
        pltpu.make_async_remote_copy(
            src_ref=source_send.at[k], dst_ref=source_recv.at[k], send_sem=send1, recv_sem=recv1.at[k],
            device_id={"src": k}, device_id_type=MESH,
        ).wait_recv()
        return k

    def forward(pair, carry):
        k = arrival(2 * pair + 1)
        later = arrival(2 * pair + 2)
        expand(k, odd_hi, odd_lo)
        correlate(even_hi, even_lo)
        expand(later, even_hi, even_lo)
        correlate(odd_hi, odd_lo)
        return carry

    lax.fori_loop(0, ns // 2 - 1, forward, 0)
    expand(arrival(ns - 1), odd_hi, odd_lo)
    correlate(even_hi, even_lo)
    correlate(odd_hi, odd_lo)

    gram = gram_hh[...] + 2.0 * gram_hl[...]
    even = gram[:LANES, :LANES] + gram[LANES:, LANES:]
    odd = gram[LANES:, :LANES] - gram[:LANES, LANES:]
    vis_re = 0.5 * (even + even.T)
    vis_im = 0.5 * (odd - odd.T)
    grid_hi, grid_lo = split(jnp.concatenate([vis_re, -vis_im], axis=0))
    grid_parts = jnp.concatenate([grid_hi, grid_lo], axis=1)

    def gather(step, carry):
        j = quad_at(s // 4, ns // 4 - 1 - step, ns // 4)
        at = pl.ds(pl.multiple_of(j * 512, 512), 512)
        picked = dot(grid_parts, left_twice[:, at])
        right = one_right[:, at].astype(F32)
        real = jnp.sum(picked[:LANES] * right, axis=0, keepdims=True)
        imag = jnp.sum(picked[LANES:] * right, axis=0, keepdims=True)
        for i in range(4):
            peer = j * 4 + i
            vis_send[peer, 0:1, :] = real[:, i * LANES : (i + 1) * LANES]
            vis_send[peer, 1:2, :] = imag[:, i * LANES : (i + 1) * LANES]

            @pl.when(peer != s)
            def _():
                pltpu.make_async_remote_copy(
                    src_ref=vis_send.at[peer], dst_ref=vis_recv.at[s], send_sem=send3, recv_sem=recv3,
                    device_id={"src": peer}, device_id_type=MESH,
                ).start()

        return carry

    lax.fori_loop(0, ns // 4, gather, 0)
    vis_recv[s] = vis_send[s]

    @pl.when(q == centre)
    def _():
        def take_data(step, carry):
            other = lax.rem(q + step, nf)
            pltpu.make_async_remote_copy(
                src_ref=data_ref, dst_ref=dat_recv.at[other], send_sem=send2, recv_sem=recv2.at[other],
                device_id={"freq": other}, device_id_type=MESH,
            ).wait_recv()
            return carry

        lax.fori_loop(1, nf, take_data, 0)

    most = pl.ds(0, ns - 1)
    pltpu.make_async_copy(vis_send.at[most], vis_recv.at[most], recv3).wait()
    for i in range(ns):
        vis_rows[2 * i : 2 * i + 2, :] = vis_recv[i]

    @pl.when(q != centre)
    def _():
        pltpu.make_async_remote_copy(
            src_ref=vis_rows, dst_ref=vis_all.at[q], send_sem=send4, recv_sem=recv4.at[q],
            device_id={"freq": centre}, device_id_type=MESH,
        ).start()

    @pl.when(q == centre)
    def _():
        vis_all[q] = vis_rows[...]

        def three_passes(i, high, low):
            both = dot(tables_hi[i], jnp.concatenate([high, low], axis=1))
            return both[:, :LANES] + both[:, LANES:] + dot(tables_lo[i], high)

        weight = jnp.transpose(jnp.broadcast_to(dw_ref[...], (LANES, nch)))
        spectra = [
            jnp.transpose(jnp.concatenate([dat_recv[i, c] for i in range(nf)], axis=0)) for c in range(2)
        ]

        def take_vis(step, carry):
            other = lax.rem(q + step, nf)
            pltpu.make_async_remote_copy(
                src_ref=vis_rows, dst_ref=vis_all.at[other], send_sem=send4, recv_sem=recv4.at[other],
                device_id={"freq": other}, device_id_type=MESH,
            ).wait_recv()
            return carry

        lax.fori_loop(1, nf, take_vis, 0)
        vis_hi, vis_lo = split(jnp.concatenate([vis_all[i] for i in range(nf)], axis=0))
        spec = three_passes(0, vis_hi, vis_lo)
        spec_cot = jnp.concatenate(
            [weight * (spec[:nch] - spectra[0]), weight * (spec[nch:] - spectra[1])], axis=0
        )
        cot_hi, cot_lo = split(spec_cot)
        back = three_passes(1, cot_hi, cot_lo)
        for i in range(nf):
            cot_all[i] = back[i * rows : (i + 1) * rows]

        def send_cot(step, carry):
            other = lax.rem(q + step, nf)
            pltpu.make_async_remote_copy(
                src_ref=cot_all.at[other], dst_ref=cot_rows, send_sem=send5, recv_sem=recv5,
                device_id={"freq": other}, device_id_type=MESH,
            ).start()
            return carry

        lax.fori_loop(1, nf, send_cot, 0)
        cot_rows[...] = cot_all[q]

    @pl.when(q != centre)
    def _():
        pltpu.make_async_remote_copy(
            src_ref=cot_all.at[q], dst_ref=cot_rows, send_sem=send5, recv_sem=recv5,
            device_id={"freq": centre}, device_id_type=MESH,
        ).wait_recv()

    for i in range(ns):
        cot_send[i] = cot_rows[2 * i : 2 * i + 2, :]

    def fan_out(step, carry):
        peer = peer_at(s, ns - step, ns)
        pltpu.make_async_remote_copy(
            src_ref=cot_send.at[peer], dst_ref=cot_recv.at[s], send_sem=send6, recv_sem=recv6.at[s // 4],
            device_id={"src": peer}, device_id_type=MESH,
        ).start()
        return carry

    lax.fori_loop(1, ns, fan_out, 0)
    cot_recv[s] = cot_send[s]

    def scatter(step, total):
        j = quad_at(s // 4, step, ns // 4)

        @pl.when(step == 0)
        def _():
            pltpu.make_async_copy(cot_send.at[pl.ds(0, 3)], cot_recv.at[pl.ds(0, 3)], recv6.at[j]).wait()

        @pl.when(step != 0)
        def _():
            pltpu.make_async_copy(cot_send.at[pl.ds(0, 4)], cot_recv.at[pl.ds(0, 4)], recv6.at[j]).wait()

        at = pl.ds(pl.multiple_of(j * 512, 512), 512)
        right = one_right[:, at]
        parts = []
        for c in range(2):
            row = jnp.concatenate([cot_recv[j * 4 + i, c : c + 1, :] for i in range(4)], axis=1)
            parts.append(split(row))
        scaled = [right * parts[c][part] for part in range(2) for c in range(2)]
        return total + dot(left_twice[:LANES, at], jnp.concatenate(scaled, axis=0), NT)

    grids = lax.fori_loop(0, ns // 4, scatter, jnp.zeros((LANES, 4 * LANES), F32))
    grids = grids[:, : 2 * LANES] + grids[:, 2 * LANES :]
    real, imag = grids[:, :LANES], grids[:, LANES:]
    real, imag = 0.5 * (real + real.T), 0.5 * (imag - imag.T)
    matrix = jnp.concatenate(
        [jnp.concatenate([real, -imag], axis=1), jnp.concatenate([imag, real], axis=1)], axis=0
    )
    matrix_hi, matrix_lo = split(matrix)

    def pull_back(k):
        for lane in range(0, slots, 256):
            at = pl.ds(lane, 256)
            high = phased_hi[k, :, at]
            product = dot(matrix_hi, high) + dot(matrix_lo, high)
            phased = high.astype(F32) + 2.0 * phased_lo[k, :, at].astype(F32)
            u_send[k, :, at] = jnp.sum(phased * product, axis=0, keepdims=True)

    def send_gradient(k):
        pltpu.make_async_remote_copy(
            src_ref=u_send.at[k], dst_ref=u_recv.at[s], send_sem=send7, recv_sem=recv7,
            device_id={"src": k}, device_id_type=MESH,
        ).start()

    def backward(pair, carry):
        k = peer_at(s, ns - 1 - 2 * pair, ns)
        later = peer_at(s, ns - 2 - 2 * pair, ns)
        pull_back(k)
        pull_back(later)
        send_gradient(k)
        send_gradient(later)
        return carry

    lax.fori_loop(0, ns // 2 - 1, backward, 0)
    k = peer_at(s, 1, ns)
    pull_back(k)
    send_gradient(k)
    pull_back(s)
    u_recv[s] = u_send[s]
    pltpu.make_async_copy(u_send.at[most], u_recv.at[most], recv7).wait()
    for i in range(ns):
        u_ref[i : i + 1, :] = u_recv[i]
    flux_send[0] = jnp.sum(u_ref[...], axis=0, keepdims=True)

    def send_flux(step, carry):
        other = lax.rem(q + step, nf)
        pltpu.make_async_remote_copy(
            src_ref=flux_send, dst_ref=flux_recv.at[pl.ds(q, 1)], send_sem=send8, recv_sem=recv8,
            device_id={"freq": other}, device_id_type=MESH,
        ).start()
        return carry

    lax.fori_loop(1, nf, send_flux, 0)
    flux_recv[q] = flux_send[0]
    others = pl.ds(0, nf - 1)

    pltpu.make_async_copy(source_send.at[most], source_recv.at[most], send1).wait()
    pltpu.make_async_copy(vis_send.at[most], vis_recv.at[most], send3).wait()
    pltpu.make_async_copy(cot_send.at[most], cot_recv.at[most], send6).wait()
    pltpu.make_async_copy(u_send.at[most], u_recv.at[most], send7).wait()

    @pl.when(q == centre)
    def _():
        pltpu.make_async_copy(cot_all.at[others], cot_all.at[others], send5).wait()

    @pl.when(q != centre)
    def _():
        pltpu.make_async_copy(data_ref, dat_recv.at[0], send2).wait()
        pltpu.make_async_copy(vis_rows, vis_rows, send4).wait()

    pltpu.make_async_copy(flux_recv.at[others], flux_recv.at[others], recv8).wait()
    total = flux_recv[0]
    for i in range(1, nf):
        total = total + flux_recv[i]
    total_ref[...] = total
    pltpu.make_async_copy(flux_recv.at[others], flux_recv.at[others], send8).wait()


def body(source_dirs, flux, beam, counts, antennas, pairs, data, delay_weight):
    ns, nf = lax.axis_size("src"), lax.axis_size("freq")
    slots = flux.shape[0]
    nch = ns * nf
    share = LANES // nf
    rows = 2 * ns
    vmem, hbm = pl.BlockSpec(memory_space=pltpu.VMEM), pl.BlockSpec(memory_space=pltpu.HBM)
    dma = pltpu.SemaphoreType.DMA
    macs = 4 * ns * slots * 256 * 256
    tables = jnp.asarray(delay_tables(nch))
    inputs = (
        source_dirs, flux[None, :], beam, counts, antennas, pairs, jnp.transpose(data, (0, 2, 1)),
        delay_weight[None, :], tables,
    )
    gradient, total = pl.pallas_call(
        functools.partial(kernel, ns, nf, min(3, nf - 1)),
        out_shape=(
            jax.ShapeDtypeStruct((ns, slots), F32),
            jax.ShapeDtypeStruct((1, slots), F32),
        ),
        in_specs=[hbm] * len(inputs),
        out_specs=(vmem, vmem),
        scratch_shapes=[
            (pltpu.SMEM if i == 3 else pltpu.VMEM)(value.shape, value.dtype) for i, value in enumerate(inputs)
        ] + [
            pltpu.VMEM((ns, 4, slots), F32),
            pltpu.VMEM((ns, 4, slots), F32),
            pltpu.VMEM((ns, 2 * LANES, slots), BF16),
            pltpu.VMEM((ns, 2 * LANES, slots), BF16),
            pltpu.VMEM((2 * LANES, ns * LANES), BF16),
            pltpu.VMEM((LANES, ns * LANES), BF16),
            pltpu.VMEM((LANES, LANES), BF16),
            pltpu.VMEM((2 * LANES, slots), BF16),
            pltpu.VMEM((2 * LANES, slots), BF16),
            pltpu.VMEM((2 * LANES, slots), BF16),
            pltpu.VMEM((2 * LANES, slots), BF16),
            pltpu.VMEM((2 * LANES, 2 * LANES), F32),
            pltpu.VMEM((2 * LANES, 2 * LANES), F32),
            pltpu.VMEM((ns, 2, LANES), F32),
            pltpu.VMEM((ns, 2, LANES), F32),
            pltpu.VMEM((rows, LANES), F32),
            pltpu.VMEM((nf, rows, LANES), F32),
            pltpu.VMEM((nf, 2, share, nch), F32),
            pltpu.VMEM((2, 2 * nch, 2 * nch), BF16),
            pltpu.VMEM((2, 2 * nch, 2 * nch), BF16),
            pltpu.VMEM((nf, rows, LANES), F32),
            pltpu.VMEM((rows, LANES), F32),
            pltpu.VMEM((ns, 2, LANES), F32),
            pltpu.VMEM((ns, 2, LANES), F32),
            pltpu.VMEM((ns, 1, slots), F32),
            pltpu.VMEM((ns, 1, slots), F32),
            pltpu.VMEM((1, 1, slots), F32),
            pltpu.VMEM((nf, 1, slots), F32),
            dma((len(inputs),)),
            dma, dma((ns,)),
            dma, dma((nf,)),
            dma, dma,
            dma, dma((nf,)),
            dma, dma,
            dma, dma((ns // 4,)),
            dma, dma,
            dma, dma,
        ],
        compiler_params=pltpu.CompilerParams(
            collective_id=0, has_side_effects=True, vmem_limit_bytes=63 * 1024 * 1024
        ),
        cost_estimate=pl.CostEstimate(flops=2 * macs, bytes_accessed=4 * 1024 * 1024, transcendentals=0),
    )(*inputs)
    return (total[0] / flux, 2.0 * gradient / beam)


def solution(mesh):
    in_specs = (
        P(None, "src"),
        P("src"),
        P("freq", "src"),
        P(),
        P(),
        P(),
        P(None, None, ("src", "freq")),
        P(),
    )
    out_specs = (P("src"), P("freq", "src"))
    return jax.shard_map(body, mesh=mesh, in_specs=in_specs, out_specs=out_specs, check_vma=False)
```

```python
import functools
import math

import jax
import jax.numpy as jnp
import numpy as np
from jax import lax
from jax.experimental import pallas as pl
from jax.experimental.pallas import tpu as pltpu
from jax.sharding import PartitionSpec as P

TWO_PI = 2.0 * math.pi
MESH = pl.DeviceIdType.MESH
F32 = jnp.float32
BF16 = jnp.bfloat16
LANES = 128
NT = (((1,), (1,)), ((), ()))
NN = (((1,), (0,)), ((), ()))
SIN_POLY = (3.1415902702069913, -5.167406733272317, 2.544010518503151, -0.5594624554674011)
COS_POLY = (0.9999999532476082, -4.93479283061961, 4.058411352862035, -1.3318765680776314, 0.2196896110917421)


def dot(left, right, dims=NN):
    return lax.dot_general(left, right, dims, preferred_element_type=F32)


def split(value):
    high = value.astype(BF16)
    return high, (value - high.astype(F32)).astype(BF16)


def horner(coefficients, variable):
    total = coefficients[-1] * variable + coefficients[-2]
    for coefficient in coefficients[-3::-1]:
        total = total * variable + coefficient
    return total


def scaled_cos_sin(turns, root):
    rest = turns - jnp.round(turns)
    square = rest * rest
    sine = rest * horner(SIN_POLY, square)
    twice = (2.0 * root) * sine
    return root - twice * sine, twice * horner(COS_POLY, square)


def three_parts(value):
    first = value.astype(BF16).astype(F32)
    rest = value - first
    second = rest.astype(BF16).astype(F32)
    return first, second, (rest - second).astype(BF16).astype(F32)


def delay_tables(nch):
    index = np.arange(nch)
    angle = 2.0 * np.pi * ((index[:, None] * index[None, :]) % nch) / nch
    taper = 0.6 - 0.4 * np.cos(2.0 * np.pi * (index + 0.5) / nch)
    cos, sin = np.cos(angle) / math.sqrt(nch), np.sin(angle) / math.sqrt(nch)
    forward = np.zeros((2, nch, nch, 2))
    forward[0, :, :, 0] = cos
    forward[0, :, :, 1] = sin
    forward[1, :, :, 0] = -sin
    forward[1, :, :, 1] = cos
    forward *= taper[None, None, :, None]
    forward = forward.reshape(2 * nch, 2 * nch)
    return np.stack([forward, forward.T]).astype(np.float32)


def peer_at(own, step, count):
    if count != 32:
        return lax.rem(own + step, count)
    own_x, own_z, own_y = lax.rem(own, 4), lax.rem(own // 4, 2), own // 8
    x = lax.rem(own_x + lax.rem(step, 4), 4)
    y = lax.rem(own_y + lax.rem(step // 4, 4), 4)
    z = lax.rem(own_z + step // 16, 2)
    return y * 8 + z * 4 + x


def quad_at(own, step, count):
    if count != 8:
        return lax.rem(own + step, count)
    y = lax.rem(own // 2 + lax.rem(step, 4), 4)
    z = lax.rem(lax.rem(own, 2) + step // 4, 2)
    return y * 2 + z


def kernel(
    ns, nf, centre,
    dirs_hbm, flux_hbm, beam_hbm, counts_hbm, ant_hbm, pairs_hbm, data_hbm, dw_hbm, tables_hbm,
    u_ref, total_ref,
    dirs_ref, flux_ref, beam_ref, counts_ref, ant_ref, pairs_ref, data_ref, dw_ref, tables,
    source_send, source_recv, phased_hi, phased_lo, phased_sum, left_twice, one_right, ant_parts, even_hi, even_lo, odd_hi, odd_lo, gram_hh, gram_hl,
    vis_send, vis_recv, vis_rows, vis_all, dat_recv, tables_hi, tables_lo, cot_all, cot_rows, cot_send, cot_recv,
    u_send, u_recv, flux_send, flux_recv,
    input_sem, send1, recv1, send2, recv2, send3, recv3, send4, recv4, send5, recv5, send6, recv6, send7, recv7,
    send8, recv8,
):
    nch = ns * nf
    slots = dirs_ref.shape[1]
    nb = ns * LANES
    rows = 2 * ns
    s = lax.axis_index("src")
    q = lax.axis_index("freq")

    inputs = [
        pltpu.make_async_copy(hbm, vmem, input_sem.at[i])
        for i, (hbm, vmem) in enumerate((
            (dirs_hbm, dirs_ref), (flux_hbm, flux_ref), (beam_hbm, beam_ref), (counts_hbm, counts_ref),
            (ant_hbm, ant_ref), (pairs_hbm, pairs_ref), (data_hbm, data_ref), (dw_hbm, dw_ref),
            (tables_hbm, tables),
        ))
    ]
    for copy in inputs:
        copy.start()
    barrier = pltpu.get_barrier_semaphore()

    def greet_src(step, carry):
        pl.semaphore_signal(barrier, inc=1, device_id={"src": peer_at(s, ns - step, ns)}, device_id_type=MESH)
        return carry

    def greet_freq(step, carry):
        pl.semaphore_signal(barrier, inc=1, device_id={"freq": lax.rem(q + step, nf)}, device_id_type=MESH)
        return carry

    lax.fori_loop(1, ns, greet_src, 0)
    lax.fori_loop(1, nf, greet_freq, 0)
    for copy in inputs[:8]:
        copy.wait()

    along_l, along_m = dirs_ref[0:1, :], dirs_ref[1:2, :]
    along_n = jnp.sqrt(1.0 - along_l * along_l - along_m * along_m)
    live = lax.broadcasted_iota(jnp.int32, (1, slots), 1) < counts_ref[s]
    strength = jnp.where(live, jnp.sqrt(flux_ref[...] * (1.0 / math.sqrt(slots * ns))), 0.0)
    roots = beam_ref[...] * strength
    for i in range(ns):
        source_send[i, 0:1, :] = along_l
        source_send[i, 1:2, :] = along_m
        source_send[i, 2:3, :] = along_n
        source_send[i, 3:4, :] = roots[i : i + 1, :]
    source_recv[s] = source_send[s]

    freq = 1.0 + 0.6 * (q * ns + s).astype(F32) / nch
    first, second, third = three_parts(
        jnp.concatenate([ant_ref[...] * freq, jnp.zeros((5, LANES), F32)], axis=0)
    )
    spare = jnp.zeros((LANES - 48, LANES), F32)
    ant_parts[...] = jnp.transpose(
        jnp.concatenate([first, second, third, first, second, first, spare], axis=0)
    ).astype(BF16)

    gram_hh[...] = jnp.zeros_like(gram_hh)
    gram_hl[...] = jnp.zeros_like(gram_hl)

    def expand(k, high_ref, low_ref):
        source = jnp.concatenate([source_recv[k], jnp.zeros((4, slots), F32)], axis=0)
        first, second, third = three_parts(source)
        parts = jnp.concatenate([first, first, first, second, second, third], axis=0).astype(BF16)
        turns = dot(ant_parts[:, :48], parts)
        for lane in range(0, slots, LANES):
            root = source_recv[k, 3:4, pl.ds(lane, LANES)]
            for top in range(0, LANES, 64):
                cosine, sine = scaled_cos_sin(turns[top : top + 64, lane : lane + LANES], root)
                for base, value in ((0, cosine), (LANES, sine)):
                    high, low = split(value)
                    at = (pl.ds(base + top, 64), pl.ds(lane, LANES))
                    phased_hi[(k, *at)] = high
                    phased_lo[(k, *at)] = low
                    high_ref[at] = high
                    low_ref[at] = low

    def correlate(high_ref, low_ref):
        high = high_ref[...]
        gram_hh[...] += dot(high, high, NT)
        gram_hl[...] += dot(high, low_ref[...], NT)

    odd_hi[...] = jnp.zeros_like(odd_hi)
    odd_lo[...] = jnp.zeros_like(odd_lo)

    antenna_id = lax.broadcasted_iota(jnp.int32, (LANES, 512), 0)

    def build_one_hot(j, carry):
        at = pl.ds(pl.multiple_of(j * 512, 512), 512)
        left = (antenna_id == pairs_ref[0:1, at]).astype(F32).astype(BF16)
        left_twice[:LANES, at] = left
        left_twice[LANES:, at] = left
        one_right[:, at] = (antenna_id == pairs_ref[1:2, at]).astype(F32).astype(BF16)
        return carry

    lax.fori_loop(0, nb // 512, build_one_hot, 0)
    inputs[8].wait()

    @pl.when(q == centre)
    def _():
        piece = min(64, 2 * nch)

        def split_tables(j, carry):
            at = pl.ds(pl.multiple_of(j * piece, piece), piece)
            for i in range(2):
                tables_hi[i, at, :], tables_lo[i, at, :] = split(tables[i, at, :])
            return carry

        lax.fori_loop(0, 2 * nch // piece, split_tables, 0)

    pl.semaphore_wait(barrier, ns - 1 + nf - 1)

    def send_sources(step, carry):
        peer = peer_at(s, ns - step, ns)
        pltpu.make_async_remote_copy(
            src_ref=source_send.at[peer], dst_ref=source_recv.at[s], send_sem=send1, recv_sem=recv1.at[s // 4],
            device_id={"src": peer}, device_id_type=MESH,
        ).start()
        return carry

    lax.fori_loop(1, ns, send_sources, 0)

    @pl.when(q == centre)
    def _():
        dat_recv[q] = data_ref[...]

    @pl.when(q != centre)
    def _():
        pltpu.make_async_remote_copy(
            src_ref=data_ref, dst_ref=dat_recv.at[q], send_sem=send2, recv_sem=recv2.at[q],
            device_id={"freq": centre}, device_id_type=MESH,
        ).start()

    def forward(step, carry):
        j = quad_at(s // 4, step, ns // 4)

        @pl.when(step == 0)
        def _():
            at = pl.ds(0, 3)
            pltpu.make_async_copy(source_send.at[at], source_recv.at[at], recv1.at[j]).wait()

        @pl.when(step != 0)
        def _():
            at = pl.ds(0, 4)
            pltpu.make_async_copy(source_send.at[at], source_recv.at[at], recv1.at[j]).wait()

        expand(j * 4, even_hi, even_lo)
        correlate(odd_hi, odd_lo)
        expand(j * 4 + 1, odd_hi, odd_lo)
        correlate(even_hi, even_lo)
        expand(j * 4 + 2, even_hi, even_lo)
        correlate(odd_hi, odd_lo)
        expand(j * 4 + 3, odd_hi, odd_lo)
        correlate(even_hi, even_lo)
        return carry

    lax.fori_loop(0, ns // 4, forward, 0)
    correlate(odd_hi, odd_lo)

    gram = gram_hh[...] + 2.0 * gram_hl[...]
    even = gram[:LANES, :LANES] + gram[LANES:, LANES:]
    odd = gram[LANES:, :LANES] - gram[:LANES, LANES:]
    vis_re = 0.5 * (even + even.T)
    vis_im = 0.5 * (odd - odd.T)
    grid_hi, grid_lo = split(jnp.concatenate([vis_re, -vis_im], axis=0))
    grid_parts = jnp.concatenate([grid_hi, grid_lo], axis=1)

    def gather(step, carry):
        j = quad_at(s // 4, ns // 4 - 1 - step, ns // 4)
        at = pl.ds(pl.multiple_of(j * 512, 512), 512)
        picked = dot(grid_parts, left_twice[:, at])
        right = one_right[:, at].astype(F32)
        real = jnp.sum(picked[:LANES] * right, axis=0, keepdims=True)
        imag = jnp.sum(picked[LANES:] * right, axis=0, keepdims=True)
        for i in range(4):
            peer = j * 4 + i
            vis_send[peer, 0:1, :] = real[:, i * LANES : (i + 1) * LANES]
            vis_send[peer, 1:2, :] = imag[:, i * LANES : (i + 1) * LANES]

            @pl.when(peer != s)
            def _():
                pltpu.make_async_remote_copy(
                    src_ref=vis_send.at[peer], dst_ref=vis_recv.at[s], send_sem=send3, recv_sem=recv3,
                    device_id={"src": peer}, device_id_type=MESH,
                ).start()

        return carry

    lax.fori_loop(0, ns // 4, gather, 0)
    vis_recv[s] = vis_send[s]

    @pl.when(q == centre)
    def _():
        def take_data(step, carry):
            other = lax.rem(q + step, nf)
            pltpu.make_async_remote_copy(
                src_ref=data_ref, dst_ref=dat_recv.at[other], send_sem=send2, recv_sem=recv2.at[other],
                device_id={"freq": other}, device_id_type=MESH,
            ).wait_recv()
            return carry

        lax.fori_loop(1, nf, take_data, 0)

    def add_parts(k, carry):
        for top in range(0, 2 * LANES, 64):
            at = pl.ds(top, 64)
            phased_sum[k, at, :] = phased_hi[k, at, :].astype(F32) + 2.0 * phased_lo[k, at, :].astype(F32)
        return carry

    lax.fori_loop(0, ns, add_parts, 0)
    most = pl.ds(0, ns - 1)
    pltpu.make_async_copy(vis_send.at[most], vis_recv.at[most], recv3).wait()
    for i in range(ns):
        vis_rows[2 * i : 2 * i + 2, :] = vis_recv[i]

    @pl.when(q != centre)
    def _():
        pltpu.make_async_remote_copy(
            src_ref=vis_rows, dst_ref=vis_all.at[q], send_sem=send4, recv_sem=recv4.at[q],
            device_id={"freq": centre}, device_id_type=MESH,
        ).start()

    @pl.when(q == centre)
    def _():
        vis_all[q] = vis_rows[...]

        def three_passes(i, high, low):
            both = dot(tables_hi[i], jnp.concatenate([high, low], axis=1))
            return both[:, :LANES] + both[:, LANES:] + dot(tables_lo[i], high)

        weight = jnp.transpose(jnp.broadcast_to(dw_ref[...], (LANES, nch)))
        spectra = [
            jnp.transpose(jnp.concatenate([dat_recv[i, c] for i in range(nf)], axis=0)) for c in range(2)
        ]

        def take_vis(step, carry):
            other = lax.rem(q + step, nf)
            pltpu.make_async_remote_copy(
                src_ref=vis_rows, dst_ref=vis_all.at[other], send_sem=send4, recv_sem=recv4.at[other],
                device_id={"freq": other}, device_id_type=MESH,
            ).wait_recv()
            return carry

        lax.fori_loop(1, nf, take_vis, 0)
        vis_hi, vis_lo = split(jnp.concatenate([vis_all[i] for i in range(nf)], axis=0))
        spec = three_passes(0, vis_hi, vis_lo)
        spec_cot = jnp.concatenate(
            [weight * (spec[:nch] - spectra[0]), weight * (spec[nch:] - spectra[1])], axis=0
        )
        cot_hi, cot_lo = split(spec_cot)
        back = three_passes(1, cot_hi, cot_lo)
        for i in range(nf):
            cot_all[i] = back[i * rows : (i + 1) * rows]

        def send_cot(step, carry):
            other = lax.rem(q + step, nf)
            pltpu.make_async_remote_copy(
                src_ref=cot_all.at[other], dst_ref=cot_rows, send_sem=send5, recv_sem=recv5,
                device_id={"freq": other}, device_id_type=MESH,
            ).start()
            return carry

        lax.fori_loop(1, nf, send_cot, 0)
        cot_rows[...] = cot_all[q]

    @pl.when(q != centre)
    def _():
        pltpu.make_async_remote_copy(
            src_ref=cot_all.at[q], dst_ref=cot_rows, send_sem=send5, recv_sem=recv5,
            device_id={"freq": centre}, device_id_type=MESH,
        ).wait_recv()

    for i in range(ns):
        cot_send[i] = cot_rows[2 * i : 2 * i + 2, :]

    def fan_out(step, carry):
        peer = peer_at(s, ns - step, ns)
        pltpu.make_async_remote_copy(
            src_ref=cot_send.at[peer], dst_ref=cot_recv.at[s], send_sem=send6, recv_sem=recv6.at[s // 4],
            device_id={"src": peer}, device_id_type=MESH,
        ).start()
        return carry

    lax.fori_loop(1, ns, fan_out, 0)
    cot_recv[s] = cot_send[s]

    def scatter(step, total):
        j = quad_at(s // 4, step, ns // 4)

        @pl.when(step == 0)
        def _():
            pltpu.make_async_copy(cot_send.at[pl.ds(0, 3)], cot_recv.at[pl.ds(0, 3)], recv6.at[j]).wait()

        @pl.when(step != 0)
        def _():
            pltpu.make_async_copy(cot_send.at[pl.ds(0, 4)], cot_recv.at[pl.ds(0, 4)], recv6.at[j]).wait()

        at = pl.ds(pl.multiple_of(j * 512, 512), 512)
        right = one_right[:, at]
        parts = []
        for c in range(2):
            row = jnp.concatenate([cot_recv[j * 4 + i, c : c + 1, :] for i in range(4)], axis=1)
            parts.append(split(row))
        scaled = [right * parts[c][part] for part in range(2) for c in range(2)]
        return total + dot(left_twice[:LANES, at], jnp.concatenate(scaled, axis=0), NT)

    grids = lax.fori_loop(0, ns // 4, scatter, jnp.zeros((LANES, 4 * LANES), F32))
    grids = grids[:, : 2 * LANES] + grids[:, 2 * LANES :]
    real, imag = grids[:, :LANES], grids[:, LANES:]
    real, imag = 0.5 * (real + real.T), 0.5 * (imag - imag.T)
    matrix = jnp.concatenate(
        [jnp.concatenate([real, -imag], axis=1), jnp.concatenate([imag, real], axis=1)], axis=0
    )
    matrix_parts = jnp.concatenate(split(matrix), axis=0)

    def pull_back(k):
        for lane in range(0, slots, 256):
            at = pl.ds(lane, 256)
            high = phased_hi[k, :, at]
            product = dot(matrix_parts, high)
            product = product[: 2 * LANES] + product[2 * LANES :]
            u_send[k, :, at] = jnp.sum(phased_sum[k, :, at] * product, axis=0, keepdims=True)

    def backward(step, carry):
        j = quad_at(s // 4, ns // 4 - 1 - step, ns // 4)
        for i in range(4):
            pull_back(j * 4 + i)
        for i in range(4):
            peer = j * 4 + i

            @pl.when(peer != s)
            def _():
                pltpu.make_async_remote_copy(
                    src_ref=u_send.at[peer], dst_ref=u_recv.at[s], send_sem=send7, recv_sem=recv7,
                    device_id={"src": peer}, device_id_type=MESH,
                ).start()

        return carry

    lax.fori_loop(0, ns // 4, backward, 0)
    u_recv[s] = u_send[s]
    pltpu.make_async_copy(u_send.at[most], u_recv.at[most], recv7).wait()
    for i in range(ns):
        u_ref[i : i + 1, :] = u_recv[i]
    flux_send[0] = jnp.sum(u_ref[...], axis=0, keepdims=True)

    def send_flux(step, carry):
        other = lax.rem(q + step, nf)
        pltpu.make_async_remote_copy(
            src_ref=flux_send, dst_ref=flux_recv.at[pl.ds(q, 1)], send_sem=send8, recv_sem=recv8,
            device_id={"freq": other}, device_id_type=MESH,
        ).start()
        return carry

    lax.fori_loop(1, nf, send_flux, 0)
    flux_recv[q] = flux_send[0]
    others = pl.ds(0, nf - 1)

    pltpu.make_async_copy(source_send.at[most], source_recv.at[most], send1).wait()
    pltpu.make_async_copy(vis_send.at[most], vis_recv.at[most], send3).wait()
    pltpu.make_async_copy(cot_send.at[most], cot_recv.at[most], send6).wait()
    pltpu.make_async_copy(u_send.at[most], u_recv.at[most], send7).wait()

    @pl.when(q == centre)
    def _():
        pltpu.make_async_copy(cot_all.at[others], cot_all.at[others], send5).wait()

    @pl.when(q != centre)
    def _():
        pltpu.make_async_copy(data_ref, dat_recv.at[0], send2).wait()
        pltpu.make_async_copy(vis_rows, vis_rows, send4).wait()

    pltpu.make_async_copy(flux_recv.at[others], flux_recv.at[others], recv8).wait()
    total = flux_recv[0]
    for i in range(1, nf):
        total = total + flux_recv[i]
    total_ref[...] = total
    pltpu.make_async_copy(flux_recv.at[others], flux_recv.at[others], send8).wait()


def body(source_dirs, flux, beam, counts, antennas, pairs, data, delay_weight):
    ns, nf = lax.axis_size("src"), lax.axis_size("freq")
    slots = flux.shape[0]
    nch = ns * nf
    share = LANES // nf
    rows = 2 * ns
    vmem, hbm = pl.BlockSpec(memory_space=pltpu.VMEM), pl.BlockSpec(memory_space=pltpu.HBM)
    dma = pltpu.SemaphoreType.DMA
    macs = 4 * ns * slots * 256 * 256
    tables = jnp.asarray(delay_tables(nch))
    inputs = (
        source_dirs, flux[None, :], beam, counts, antennas, pairs, jnp.transpose(data, (0, 2, 1)),
        delay_weight[None, :], tables,
    )
    gradient, total = pl.pallas_call(
        functools.partial(kernel, ns, nf, min(3, nf - 1)),
        out_shape=(
            pltpu.VMEM((ns, slots), F32),
            pltpu.VMEM((1, slots), F32),
        ),
        in_specs=[hbm] * len(inputs),
        out_specs=(vmem, vmem),
        scratch_shapes=[
            (pltpu.SMEM if i == 3 else pltpu.VMEM)(value.shape, value.dtype) for i, value in enumerate(inputs)
        ] + [
            pltpu.VMEM((ns, 4, slots), F32),
            pltpu.VMEM((ns, 4, slots), F32),
            pltpu.VMEM((ns, 2 * LANES, slots), BF16),
            pltpu.VMEM((ns, 2 * LANES, slots), BF16),
            pltpu.VMEM((ns, 2 * LANES, slots), F32),
            pltpu.VMEM((2 * LANES, ns * LANES), BF16),
            pltpu.VMEM((LANES, ns * LANES), BF16),
            pltpu.VMEM((LANES, LANES), BF16),
            pltpu.VMEM((2 * LANES, slots), BF16),
            pltpu.VMEM((2 * LANES, slots), BF16),
            pltpu.VMEM((2 * LANES, slots), BF16),
            pltpu.VMEM((2 * LANES, slots), BF16),
            pltpu.VMEM((2 * LANES, 2 * LANES), F32),
            pltpu.VMEM((2 * LANES, 2 * LANES), F32),
            pltpu.VMEM((ns, 2, LANES), F32),
            pltpu.VMEM((ns, 2, LANES), F32),
            pltpu.VMEM((rows, LANES), F32),
            pltpu.VMEM((nf, rows, LANES), F32),
            pltpu.VMEM((nf, 2, share, nch), F32),
            pltpu.VMEM((2, 2 * nch, 2 * nch), BF16),
            pltpu.VMEM((2, 2 * nch, 2 * nch), BF16),
            pltpu.VMEM((nf, rows, LANES), F32),
            pltpu.VMEM((rows, LANES), F32),
            pltpu.VMEM((ns, 2, LANES), F32),
            pltpu.VMEM((ns, 2, LANES), F32),
            pltpu.VMEM((ns, 1, slots), F32),
            pltpu.VMEM((ns, 1, slots), F32),
            pltpu.VMEM((1, 1, slots), F32),
            pltpu.VMEM((nf, 1, slots), F32),
            dma((len(inputs),)),
            dma, dma((ns // 4,)),
            dma, dma((nf,)),
            dma, dma,
            dma, dma((nf,)),
            dma, dma,
            dma, dma((ns // 4,)),
            dma, dma,
            dma, dma,
        ],
        compiler_params=pltpu.CompilerParams(
            collective_id=0, has_side_effects=True, vmem_limit_bytes=63 * 1024 * 1024
        ),
        cost_estimate=pl.CostEstimate(flops=2 * macs, bytes_accessed=4 * 1024 * 1024, transcendentals=0),
    )(*inputs)
    return (total[0] / flux, 2.0 * gradient / beam)


def solution(mesh):
    in_specs = (
        P(None, "src"),
        P("src"),
        P("freq", "src"),
        P(),
        P(),
        P(),
        P(None, None, ("src", "freq")),
        P(),
    )
    out_specs = (P("src"), P("freq", "src"))
    return jax.shard_map(body, mesh=mesh, in_specs=in_specs, out_specs=out_specs, check_vma=False)
```

```python
import functools
import math

import jax
import jax.numpy as jnp
import numpy as np
from jax import lax
from jax.experimental import pallas as pl
from jax.experimental.pallas import tpu as pltpu
from jax.sharding import PartitionSpec as P

TWO_PI = 2.0 * math.pi
MESH = pl.DeviceIdType.MESH
F32 = jnp.float32
BF16 = jnp.bfloat16
LANES = 128
NT = (((1,), (1,)), ((), ()))
NN = (((1,), (0,)), ((), ()))
SIN_POLY = (3.1415902702069913, -5.167406733272317, 2.544010518503151, -0.5594624554674011)
COS_POLY = (0.9999999532476082, -4.93479283061961, 4.058411352862035, -1.3318765680776314, 0.2196896110917421)


def dot(left, right, dims=NN):
    return lax.dot_general(left, right, dims, preferred_element_type=F32)


def split(value):
    high = value.astype(BF16)
    return high, (value - high.astype(F32)).astype(BF16)


def horner(coefficients, variable):
    total = coefficients[-1] * variable + coefficients[-2]
    for coefficient in coefficients[-3::-1]:
        total = total * variable + coefficient
    return total


def scaled_cos_sin(turns, root):
    rest = turns - jnp.round(turns)
    square = rest * rest
    sine = rest * horner(SIN_POLY, square)
    twice = (2.0 * root) * sine
    return root - twice * sine, twice * horner(COS_POLY, square)


def three_parts(value):
    first = value.astype(BF16).astype(F32)
    rest = value - first
    second = rest.astype(BF16).astype(F32)
    return first, second, (rest - second).astype(BF16).astype(F32)


def delay_tables(nch):
    index = np.arange(nch)
    angle = 2.0 * np.pi * ((index[:, None] * index[None, :]) % nch) / nch
    taper = 0.6 - 0.4 * np.cos(2.0 * np.pi * (index + 0.5) / nch)
    cos, sin = np.cos(angle) / math.sqrt(nch), np.sin(angle) / math.sqrt(nch)
    forward = np.zeros((2, nch, nch, 2))
    forward[0, :, :, 0] = cos
    forward[0, :, :, 1] = sin
    forward[1, :, :, 0] = -sin
    forward[1, :, :, 1] = cos
    forward *= taper[None, None, :, None]
    forward = forward.reshape(2 * nch, 2 * nch)
    return np.stack([forward, forward.T]).astype(np.float32)


def peer_at(own, step, count):
    if count != 32:
        return lax.rem(own + step, count)
    own_x, own_z, own_y = lax.rem(own, 4), lax.rem(own // 4, 2), own // 8
    x = lax.rem(own_x + lax.rem(step, 4), 4)
    y = lax.rem(own_y + lax.rem(step // 4, 4), 4)
    z = lax.rem(own_z + step // 16, 2)
    return y * 8 + z * 4 + x


def quad_at(own, step, count):
    if count != 8:
        return lax.rem(own + step, count)
    y = lax.rem(own // 2 + lax.rem(step, 4), 4)
    z = lax.rem(lax.rem(own, 2) + step // 4, 2)
    return y * 2 + z


def kernel(
    ns, nf, centre,
    dirs_hbm, flux_hbm, beam_hbm, counts_hbm, ant_hbm, pairs_hbm, data_hbm, dw_hbm, tables_hbm,
    u_ref, total_ref,
    dirs_ref, flux_ref, beam_ref, counts_ref, ant_ref, pairs_ref, data_ref, dw_ref, tables,
    source_send, source_recv, phased_hi, phased_lo, phased_sum, left_twice, one_right, ant_parts, even_hi, even_lo, odd_hi, odd_lo, gram_hh, gram_hl,
    vis_send, vis_all, vis_rows, dat_recv, tables_hi, tables_lo, cot_all, cot_recv,
    u_send, u_recv, flux_send, flux_recv,
    input_sem, send1, recv1, send2, recv2, send3, recv3, send6, recv6, send7, recv7,
    send8, recv8,
):
    nch = ns * nf
    slots = dirs_ref.shape[1]
    nb = ns * LANES
    quads = ns // 4
    s = lax.axis_index("src")
    q = lax.axis_index("freq")

    inputs = [
        pltpu.make_async_copy(hbm, vmem, input_sem.at[i])
        for i, (hbm, vmem) in enumerate((
            (dirs_hbm, dirs_ref), (flux_hbm, flux_ref), (beam_hbm, beam_ref), (counts_hbm, counts_ref),
            (ant_hbm, ant_ref), (pairs_hbm, pairs_ref), (data_hbm, data_ref), (dw_hbm, dw_ref),
            (tables_hbm, tables),
        ))
    ]
    for copy in inputs:
        copy.start()
    barrier = pltpu.get_barrier_semaphore()

    def greet(peer, group):
        pl.semaphore_signal(barrier, inc=1, device_id={"src": peer, "freq": group}, device_id_type=MESH)

    def greet_quad(step, carry):
        j = quad_at(s // 4, quads - 1 - step, quads)
        for i in range(4):
            peer = j * 4 + i

            @pl.when(peer != s)
            def _():
                greet(peer, q)

                @pl.when(q != centre)
                def _():
                    greet(peer, centre)

                @pl.when(q == centre)
                def _():
                    for group in range(nf):
                        if group != centre:
                            greet(peer, group)

        return carry

    def greet_freq(step, carry):
        greet(s, lax.rem(q + step, nf))
        return carry

    lax.fori_loop(0, quads, greet_quad, 0)
    lax.fori_loop(1, nf, greet_freq, 0)
    for copy in inputs[:8]:
        copy.wait()

    along_l, along_m = dirs_ref[0:1, :], dirs_ref[1:2, :]
    along_n = jnp.sqrt(1.0 - along_l * along_l - along_m * along_m)
    live = lax.broadcasted_iota(jnp.int32, (1, slots), 1) < counts_ref[s]
    strength = jnp.where(live, jnp.sqrt(flux_ref[...] * (1.0 / math.sqrt(slots * ns))), 0.0)
    roots = beam_ref[...] * strength
    for i in range(ns):
        source_send[i, 0:1, :] = along_l
        source_send[i, 1:2, :] = along_m
        source_send[i, 2:3, :] = along_n
        source_send[i, 3:4, :] = roots[i : i + 1, :]
    source_recv[s] = source_send[s]

    freq = 1.0 + 0.6 * (q * ns + s).astype(F32) / nch
    first, second, third = three_parts(
        jnp.concatenate([ant_ref[...] * freq, jnp.zeros((5, LANES), F32)], axis=0)
    )
    spare = jnp.zeros((LANES - 48, LANES), F32)
    ant_parts[...] = jnp.transpose(
        jnp.concatenate([first, second, third, first, second, first, spare], axis=0)
    ).astype(BF16)

    gram_hh[...] = jnp.zeros_like(gram_hh)
    gram_hl[...] = jnp.zeros_like(gram_hl)

    def expand(k, high_ref, low_ref):
        source = jnp.concatenate([source_recv[k], jnp.zeros((4, slots), F32)], axis=0)
        first, second, third = three_parts(source)
        parts = jnp.concatenate([first, first, first, second, second, third], axis=0).astype(BF16)
        turns = dot(ant_parts[:, :48], parts)
        for lane in range(0, slots, LANES):
            root = source_recv[k, 3:4, pl.ds(lane, LANES)]
            for top in range(0, LANES, 64):
                cosine, sine = scaled_cos_sin(turns[top : top + 64, lane : lane + LANES], root)
                for base, value in ((0, cosine), (LANES, sine)):
                    high, low = split(value)
                    at = (pl.ds(base + top, 64), pl.ds(lane, LANES))
                    phased_hi[(k, *at)] = high
                    phased_lo[(k, *at)] = low
                    high_ref[at] = high
                    low_ref[at] = low

    def correlate(high_ref, low_ref):
        high = high_ref[...]
        gram_hh[...] += dot(high, high, NT)
        gram_hl[...] += dot(high, low_ref[...], NT)

    odd_hi[...] = jnp.zeros_like(odd_hi)
    odd_lo[...] = jnp.zeros_like(odd_lo)

    antenna_id = lax.broadcasted_iota(jnp.int32, (LANES, 512), 0)

    def build_one_hot(j, carry):
        at = pl.ds(pl.multiple_of(j * 512, 512), 512)
        left = (antenna_id == pairs_ref[0:1, at]).astype(F32).astype(BF16)
        left_twice[:LANES, at] = left
        left_twice[LANES:, at] = left
        one_right[:, at] = (antenna_id == pairs_ref[1:2, at]).astype(F32).astype(BF16)
        return carry

    lax.fori_loop(0, nb // 512, build_one_hot, 0)
    inputs[8].wait()

    @pl.when(q == centre)
    def _():
        piece = min(64, 2 * nch)

        def split_tables(j, carry):
            at = pl.ds(pl.multiple_of(j * piece, piece), piece)
            for i in range(2):
                tables_hi[i, at, :], tables_lo[i, at, :] = split(tables[i, at, :])
            return carry

        lax.fori_loop(0, 2 * nch // piece, split_tables, 0)

    @pl.when(q == centre)
    def _():
        pl.semaphore_wait(barrier, nch - 1)

    @pl.when(q != centre)
    def _():
        pl.semaphore_wait(barrier, 2 * (ns - 1) + nf - 1)


    def send_sources(step, carry):
        j = quad_at(s // 4, step, quads)
        for i in range(4):
            peer = j * 4 + i

            @pl.when(peer != s)
            def _():
                pltpu.make_async_remote_copy(
                    src_ref=source_send.at[peer], dst_ref=source_recv.at[s], send_sem=send1,
                    recv_sem=recv1.at[s // 4], device_id={"src": peer}, device_id_type=MESH,
                ).start()

        return carry

    lax.fori_loop(0, quads, send_sources, 0)

    @pl.when(q == centre)
    def _():
        dat_recv[q] = data_ref[...]

    @pl.when(q != centre)
    def _():
        pltpu.make_async_remote_copy(
            src_ref=data_ref, dst_ref=dat_recv.at[q], send_sem=send2, recv_sem=recv2.at[q],
            device_id={"freq": centre}, device_id_type=MESH,
        ).start()

    def forward(step, carry):
        j = quad_at(s // 4, step, quads)

        @pl.when(step == 0)
        def _():
            at = pl.ds(0, 3)
            pltpu.make_async_copy(source_send.at[at], source_recv.at[at], recv1.at[j]).wait()

        @pl.when(step != 0)
        def _():
            at = pl.ds(0, 4)
            pltpu.make_async_copy(source_send.at[at], source_recv.at[at], recv1.at[j]).wait()

        expand(j * 4, even_hi, even_lo)
        correlate(odd_hi, odd_lo)
        expand(j * 4 + 1, odd_hi, odd_lo)
        correlate(even_hi, even_lo)
        expand(j * 4 + 2, even_hi, even_lo)
        correlate(odd_hi, odd_lo)
        expand(j * 4 + 3, odd_hi, odd_lo)
        correlate(even_hi, even_lo)
        return carry

    lax.fori_loop(0, quads, forward, 0)
    correlate(odd_hi, odd_lo)

    gram = gram_hh[...] + 2.0 * gram_hl[...]
    even = gram[:LANES, :LANES] + gram[LANES:, LANES:]
    odd = gram[LANES:, :LANES] - gram[:LANES, LANES:]
    vis_re = 0.5 * (even + even.T)
    vis_im = 0.5 * (odd - odd.T)
    grid_hi, grid_lo = split(jnp.concatenate([vis_re, -vis_im], axis=0))
    grid_parts = jnp.concatenate([grid_hi, grid_lo], axis=1)

    def gather(step, carry):
        j = quad_at(s // 4, quads - 1 - step, quads)
        at = pl.ds(pl.multiple_of(j * 512, 512), 512)
        picked = dot(grid_parts, left_twice[:, at])
        right = one_right[:, at].astype(F32)
        real = jnp.sum(picked[:LANES] * right, axis=0, keepdims=True)
        imag = jnp.sum(picked[LANES:] * right, axis=0, keepdims=True)
        for i in range(4):
            peer = j * 4 + i
            vis_send[peer, 0:1, :] = real[:, i * LANES : (i + 1) * LANES]
            vis_send[peer, 1:2, :] = imag[:, i * LANES : (i + 1) * LANES]

            @pl.when(jnp.logical_or(peer != s, q != centre))
            def _():
                pltpu.make_async_remote_copy(
                    src_ref=vis_send.at[peer], dst_ref=vis_all.at[q * ns + s], send_sem=send3, recv_sem=recv3,
                    device_id={"src": peer, "freq": centre}, device_id_type=MESH,
                ).start()

        return carry

    lax.fori_loop(0, quads, gather, 0)

    def add_parts(k, carry):
        for top in range(0, 2 * LANES, 64):
            at = pl.ds(top, 64)
            phased_sum[k, at, :] = phased_hi[k, at, :].astype(F32) + 2.0 * phased_lo[k, at, :].astype(F32)
        return carry

    lax.fori_loop(0, ns, add_parts, 0)
    most = pl.ds(0, ns - 1)
    others = pl.ds(0, nf - 1)
    all_but_one = pl.ds(0, nch - 1)

    @pl.when(q == centre)
    def _():
        def take_data(step, carry):
            other = lax.rem(q + step, nf)
            pltpu.make_async_remote_copy(
                src_ref=data_ref, dst_ref=dat_recv.at[other], send_sem=send2, recv_sem=recv2.at[other],
                device_id={"freq": other}, device_id_type=MESH,
            ).wait_recv()
            return carry

        lax.fori_loop(1, nf, take_data, 0)

        def three_passes(i, high, low):
            both = dot(tables_hi[i], jnp.concatenate([high, low], axis=1))
            return both[:, :LANES] + both[:, LANES:] + dot(tables_lo[i], high)

        weight = jnp.transpose(jnp.broadcast_to(dw_ref[...], (LANES, nch)))
        spectra = [
            jnp.transpose(jnp.concatenate([dat_recv[i, c] for i in range(nf)], axis=0)) for c in range(2)
        ]
        vis_all[q * ns + s] = vis_send[s]
        pltpu.make_async_copy(vis_all.at[all_but_one], vis_all.at[all_but_one], recv3).wait()

        def pack(j, carry):
            at = pl.ds(pl.multiple_of(j * 16, 16), 16)
            vis_rows[at, :] = jnp.concatenate([vis_all[j * 8 + i] for i in range(8)], axis=0)
            return carry

        lax.fori_loop(0, nch // 8, pack, 0)
        vis_hi, vis_lo = split(vis_rows[...])
        spec = three_passes(0, vis_hi, vis_lo)
        spec_cot = jnp.concatenate(
            [weight * (spec[:nch] - spectra[0]), weight * (spec[nch:] - spectra[1])], axis=0
        )
        cot_hi, cot_lo = split(spec_cot)
        vis_rows[...] = three_passes(1, cot_hi, cot_lo)

        def send_cot(step, carry):
            j = quad_at(s // 4, quads - 1 - step, quads)
            for group in range(nf):
                first = group * ns + j * 4
                piece = vis_rows[pl.ds(pl.multiple_of(first * 2, 8), 8), :]
                for i in range(4):
                    peer = j * 4 + i
                    cot_all[first + i] = piece[2 * i : 2 * i + 2]

                    def send():
                        pltpu.make_async_remote_copy(
                            src_ref=cot_all.at[first + i], dst_ref=cot_recv.at[s], send_sem=send6,
                            recv_sem=recv6.at[s // 4], device_id={"src": peer, "freq": group},
                            device_id_type=MESH,
                        ).start()

                    if group == centre:
                        pl.when(peer != s)(send)
                    else:
                        send()
            return carry

        lax.fori_loop(0, quads, send_cot, 0)
        cot_recv[s] = cot_all[q * ns + s]

    def scatter(step, total):
        j = quad_at(s // 4, step, quads)

        with_own = jnp.logical_and(step == 0, q == centre)

        @pl.when(with_own)
        def _():
            pltpu.make_async_copy(cot_recv.at[pl.ds(0, 3)], cot_recv.at[pl.ds(0, 3)], recv6.at[j]).wait()

        @pl.when(jnp.logical_not(with_own))
        def _():
            pltpu.make_async_copy(cot_recv.at[pl.ds(0, 4)], cot_recv.at[pl.ds(0, 4)], recv6.at[j]).wait()

        at = pl.ds(pl.multiple_of(j * 512, 512), 512)
        right = one_right[:, at]
        parts = []
        for c in range(2):
            row = jnp.concatenate([cot_recv[j * 4 + i, c : c + 1, :] for i in range(4)], axis=1)
            parts.append(split(row))
        scaled = [right * parts[c][part] for part in range(2) for c in range(2)]
        return total + dot(left_twice[:LANES, at], jnp.concatenate(scaled, axis=0), NT)

    grids = lax.fori_loop(0, quads, scatter, jnp.zeros((LANES, 4 * LANES), F32))
    grids = grids[:, : 2 * LANES] + grids[:, 2 * LANES :]
    real, imag = grids[:, :LANES], grids[:, LANES:]
    real, imag = 0.5 * (real + real.T), 0.5 * (imag - imag.T)
    matrix = jnp.concatenate(
        [jnp.concatenate([real, -imag], axis=1), jnp.concatenate([imag, real], axis=1)], axis=0
    )
    matrix_parts = jnp.concatenate(split(matrix), axis=0)

    def pull_back(k):
        for lane in range(0, slots, 256):
            at = pl.ds(lane, 256)
            high = phased_hi[k, :, at]
            product = dot(matrix_parts, high)
            product = product[: 2 * LANES] + product[2 * LANES :]
            u_send[k, :, at] = jnp.sum(phased_sum[k, :, at] * product, axis=0, keepdims=True)

    def backward(step, carry):
        j = quad_at(s // 4, quads - 1 - step, quads)
        for i in range(4):
            pull_back(j * 4 + i)
        for i in range(4):
            peer = j * 4 + i

            @pl.when(peer != s)
            def _():
                pltpu.make_async_remote_copy(
                    src_ref=u_send.at[peer], dst_ref=u_recv.at[s], send_sem=send7, recv_sem=recv7,
                    device_id={"src": peer}, device_id_type=MESH,
                ).start()

        return carry

    lax.fori_loop(0, quads, backward, 0)
    u_recv[s] = u_send[s]
    pltpu.make_async_copy(u_send.at[most], u_recv.at[most], recv7).wait()
    for i in range(ns):
        u_ref[i : i + 1, :] = u_recv[i]
    flux_send[0] = jnp.sum(u_ref[...], axis=0, keepdims=True)

    def send_flux(step, carry):
        other = lax.rem(q + step, nf)
        pltpu.make_async_remote_copy(
            src_ref=flux_send, dst_ref=flux_recv.at[pl.ds(q, 1)], send_sem=send8, recv_sem=recv8,
            device_id={"freq": other}, device_id_type=MESH,
        ).start()
        return carry

    lax.fori_loop(1, nf, send_flux, 0)
    flux_recv[q] = flux_send[0]
    pltpu.make_async_copy(source_send.at[most], source_recv.at[most], send1).wait()
    pltpu.make_async_copy(u_send.at[most], u_recv.at[most], send7).wait()

    @pl.when(q == centre)
    def _():
        pltpu.make_async_copy(vis_send.at[most], vis_send.at[most], send3).wait()
        pltpu.make_async_copy(cot_all.at[all_but_one], cot_all.at[all_but_one], send6).wait()

    @pl.when(q != centre)
    def _():
        pltpu.make_async_copy(vis_send, vis_send, send3).wait()
        pltpu.make_async_copy(data_ref, dat_recv.at[0], send2).wait()

    pltpu.make_async_copy(flux_recv.at[others], flux_recv.at[others], recv8).wait()
    total = flux_recv[0]
    for i in range(1, nf):
        total = total + flux_recv[i]
    total_ref[...] = total
    pltpu.make_async_copy(flux_recv.at[others], flux_recv.at[others], send8).wait()


def body(source_dirs, flux, beam, counts, antennas, pairs, data, delay_weight):
    ns, nf = lax.axis_size("src"), lax.axis_size("freq")
    slots = flux.shape[0]
    nch = ns * nf
    share = LANES // nf
    vmem, hbm = pl.BlockSpec(memory_space=pltpu.VMEM), pl.BlockSpec(memory_space=pltpu.HBM)
    dma = pltpu.SemaphoreType.DMA
    macs = 4 * ns * slots * 256 * 256
    tables = jnp.asarray(delay_tables(nch))
    inputs = (
        source_dirs, flux[None, :], beam, counts, antennas, pairs, jnp.transpose(data, (0, 2, 1)),
        delay_weight[None, :], tables,
    )
    gradient, total = pl.pallas_call(
        functools.partial(kernel, ns, nf, min(3, nf - 1)),
        out_shape=(
            pltpu.VMEM((ns, slots), F32),
            pltpu.VMEM((1, slots), F32),
        ),
        in_specs=[hbm] * len(inputs),
        out_specs=(vmem, vmem),
        scratch_shapes=[
            (pltpu.SMEM if i == 3 else pltpu.VMEM)(value.shape, value.dtype) for i, value in enumerate(inputs)
        ] + [
            pltpu.VMEM((ns, 4, slots), F32),
            pltpu.VMEM((ns, 4, slots), F32),
            pltpu.VMEM((ns, 2 * LANES, slots), BF16),
            pltpu.VMEM((ns, 2 * LANES, slots), BF16),
            pltpu.VMEM((ns, 2 * LANES, slots), F32),
            pltpu.VMEM((2 * LANES, ns * LANES), BF16),
            pltpu.VMEM((LANES, ns * LANES), BF16),
            pltpu.VMEM((LANES, LANES), BF16),
            pltpu.VMEM((2 * LANES, slots), BF16),
            pltpu.VMEM((2 * LANES, slots), BF16),
            pltpu.VMEM((2 * LANES, slots), BF16),
            pltpu.VMEM((2 * LANES, slots), BF16),
            pltpu.VMEM((2 * LANES, 2 * LANES), F32),
            pltpu.VMEM((2 * LANES, 2 * LANES), F32),
            pltpu.VMEM((ns, 2, LANES), F32),
            pltpu.VMEM((nch, 2, LANES), F32),
            pltpu.VMEM((2 * nch, LANES), F32),
            pltpu.VMEM((nf, 2, share, nch), F32),
            pltpu.VMEM((2, 2 * nch, 2 * nch), BF16),
            pltpu.VMEM((2, 2 * nch, 2 * nch), BF16),
            pltpu.VMEM((nch, 2, LANES), F32),
            pltpu.VMEM((ns, 2, LANES), F32),
            pltpu.VMEM((ns, 1, slots), F32),
            pltpu.VMEM((ns, 1, slots), F32),
            pltpu.VMEM((1, 1, slots), F32),
            pltpu.VMEM((nf, 1, slots), F32),
            dma((len(inputs),)),
            dma, dma((ns // 4,)),
            dma, dma((nf,)),
            dma, dma,
            dma, dma((ns // 4,)),
            dma, dma,
            dma, dma,
        ],
        compiler_params=pltpu.CompilerParams(
            collective_id=0, has_side_effects=True, vmem_limit_bytes=63 * 1024 * 1024
        ),
        cost_estimate=pl.CostEstimate(flops=2 * macs, bytes_accessed=4 * 1024 * 1024, transcendentals=0),
    )(*inputs)
    return (total[0] / flux, 2.0 * gradient / beam)


def solution(mesh):
    in_specs = (
        P(None, "src"),
        P("src"),
        P("freq", "src"),
        P(),
        P(),
        P(),
        P(None, None, ("src", "freq")),
        P(),
    )
    out_specs = (P("src"), P("freq", "src"))
    return jax.shard_map(body, mesh=mesh, in_specs=in_specs, out_specs=out_specs, check_vma=False)
```

```python
import functools
import math

import jax
import jax.numpy as jnp
import numpy as np
from jax import lax
from jax.experimental import pallas as pl
from jax.experimental.pallas import tpu as pltpu
from jax.sharding import PartitionSpec as P

TWO_PI = 2.0 * math.pi
MESH = pl.DeviceIdType.MESH
F32 = jnp.float32
BF16 = jnp.bfloat16
LANES = 128
NT = (((1,), (1,)), ((), ()))
NN = (((1,), (0,)), ((), ()))
SIN_POLY = (3.1415902702069913, -5.167406733272317, 2.544010518503151, -0.5594624554674011)
COS_POLY = (0.9999932488527381, -4.933934668076284, 4.041248101995494, -1.2220317625317256)


def dot(left, right, dims=NN):
    return lax.dot_general(left, right, dims, preferred_element_type=F32)


def split(value):
    high = value.astype(BF16)
    return high, (value - high.astype(F32)).astype(BF16)


def horner(coefficients, variable):
    total = coefficients[-1] * variable + coefficients[-2]
    for coefficient in coefficients[-3::-1]:
        total = total * variable + coefficient
    return total


def scaled_cos_sin(turns, root):
    rest = turns - jnp.round(turns)
    square = rest * rest
    sine = rest * horner(SIN_POLY, square)
    twice = (2.0 * root) * sine
    return root - twice * sine, twice * horner(COS_POLY, square)


def three_parts(value):
    first = value.astype(BF16).astype(F32)
    rest = value - first
    second = rest.astype(BF16).astype(F32)
    return first, second, (rest - second).astype(BF16).astype(F32)


def delay_tables(nch):
    index = np.arange(nch)
    angle = 2.0 * np.pi * ((index[:, None] * index[None, :]) % nch) / nch
    taper = 0.6 - 0.4 * np.cos(2.0 * np.pi * (index + 0.5) / nch)
    cos, sin = np.cos(angle) / math.sqrt(nch), np.sin(angle) / math.sqrt(nch)
    forward = np.zeros((2, nch, nch, 2))
    forward[0, :, :, 0] = cos
    forward[0, :, :, 1] = sin
    forward[1, :, :, 0] = -sin
    forward[1, :, :, 1] = cos
    forward *= taper[None, None, :, None]
    forward = forward.reshape(2 * nch, 2 * nch)
    return np.stack([forward, forward.T]).astype(np.float32)


def in_quad(own, step):
    return own // 4 * 4 + lax.rem(own + step, 4)


def quad_at(own, step, count):
    if count != 8:
        return lax.rem(own + step, count)
    y = lax.rem(own // 2 + lax.rem(step, 4), 4)
    z = lax.rem(lax.rem(own, 2) + step // 4, 2)
    return y * 2 + z


def kernel(
    ns, nf, centre,
    dirs_hbm, flux_hbm, beam_hbm, counts_hbm, ant_hbm, pairs_hbm, data_hbm, dw_hbm, tables_hbm,
    u_ref, total_ref,
    dirs_ref, flux_ref, beam_ref, counts_ref, ant_ref, pairs_ref, data_ref, dw_ref, tables,
    source_send, source_recv, phased_hi, phased_lo, phased_sum, left_twice, one_right, ant_parts, even_hi, even_lo, odd_hi, odd_lo, gram_hh, gram_hl, grids_ref,
    vis_send, vis_all, vis_rows, dat_recv, tables_hi, tables_lo, cot_all, cot_recv,
    u_send, u_recv, flux_send, flux_recv,
    input_sem, send1, recv1, send2, recv2, send3, recv3, send6, recv6, send7, recv7,
    send8, recv8,
):
    nch = ns * nf
    slots = dirs_ref.shape[1]
    nb = ns * LANES
    quads = ns // 4
    s = lax.axis_index("src")
    q = lax.axis_index("freq")

    inputs = [
        pltpu.make_async_copy(hbm, vmem, input_sem.at[i])
        for i, (hbm, vmem) in enumerate((
            (dirs_hbm, dirs_ref), (flux_hbm, flux_ref), (beam_hbm, beam_ref), (counts_hbm, counts_ref),
            (ant_hbm, ant_ref), (pairs_hbm, pairs_ref), (data_hbm, data_ref), (dw_hbm, dw_ref),
            (tables_hbm, tables),
        ))
    ]
    for copy in inputs:
        copy.start()
    barrier = pltpu.get_barrier_semaphore()

    def greet(peer, group):
        pl.semaphore_signal(barrier, inc=1, device_id={"src": peer, "freq": group}, device_id_type=MESH)

    def greet_quad(step, carry):
        j = quad_at(s // 4, quads - 1 - step, quads)
        for i in range(4):
            peer = j * 4 + i

            @pl.when(peer != s)
            def _():
                greet(peer, q)

                @pl.when(q != centre)
                def _():
                    greet(peer, centre)

                @pl.when(q == centre)
                def _():
                    for group in range(nf):
                        if group != centre:
                            greet(peer, group)

        return carry

    def greet_freq(step, carry):
        greet(s, lax.rem(q + step, nf))
        return carry

    lax.fori_loop(0, quads, greet_quad, 0)
    lax.fori_loop(1, nf, greet_freq, 0)
    for copy in inputs[:8]:
        copy.wait()

    live = lax.broadcasted_iota(jnp.int32, (1, slots), 1) < counts_ref[s]
    strength = jnp.where(live, jnp.sqrt(flux_ref[...] * (1.0 / math.sqrt(slots * ns))), 0.0)
    roots = beam_ref[...] * strength
    along = jnp.concatenate(
        [dirs_ref[i : i + 1, pl.ds(j * LANES, LANES)] for i in range(2) for j in range(4)], axis=0
    )
    for i in range(ns):
        source_send[i, 0:8, :] = along
        for j in range(4):
            source_send[i, 8 + j : 9 + j, :] = roots[i : i + 1, j * LANES : (j + 1) * LANES]
    source_recv[s] = source_send[s]

    freq = 1.0 + 0.6 * (q * ns + s).astype(F32) / nch
    positions = jnp.concatenate(
        [jnp.broadcast_to(ant_ref[i : i + 1, :] * freq, (4, LANES)) for i in range(3)]
        + [jnp.zeros((4, LANES), F32)],
        axis=0,
    )
    row = lax.broadcasted_iota(jnp.int32, (16, LANES), 0)
    for j in range(4):
        first, second, third = three_parts(jnp.where(row % 4 == j, positions, 0.0))
        spare = jnp.zeros((LANES - 96, LANES), F32)
        ant_parts[j * LANES : (j + 1) * LANES, :] = jnp.transpose(
            jnp.concatenate([first, second, third, first, second, first, spare], axis=0)
        ).astype(BF16)

    gram_hh[...] = jnp.zeros_like(gram_hh)
    gram_hl[...] = jnp.zeros_like(gram_hl)

    def expand(k, high_ref, low_ref):
        source = source_recv[k]
        along_l, along_m = source[0:4], source[4:8]
        along_n = jnp.sqrt(1.0 - along_l * along_l - along_m * along_m)
        source = jnp.concatenate([along_l, along_m, along_n, jnp.zeros_like(along_n)], axis=0)
        first, second, third = three_parts(source)
        parts = jnp.concatenate([first, first, first, second, second, third], axis=0).astype(BF16)
        turns = dot(ant_parts[:, :96], parts)
        for lane in range(0, slots, LANES):
            piece = lane // LANES
            root = source_recv[k, 8 + piece : 9 + piece, :]
            for top in range(0, LANES, 64):
                cosine, sine = scaled_cos_sin(turns[lane + top : lane + top + 64], root)
                for base, value in ((0, cosine), (LANES, sine)):
                    high, low = split(value)
                    at = (pl.ds(base + top, 64), pl.ds(lane, LANES))
                    phased_hi[(k, *at)] = high
                    phased_lo[(k, *at)] = low
                    high_ref[at] = high
                    low_ref[at] = low

    def correlate(high_ref, low_ref):
        high = high_ref[...]
        gram_hh[...] += dot(high, high, NT)
        gram_hl[...] += dot(high, low_ref[...], NT)

    odd_hi[...] = jnp.zeros_like(odd_hi)
    odd_lo[...] = jnp.zeros_like(odd_lo)

    antenna_id = lax.broadcasted_iota(jnp.int32, (LANES, 512), 0)

    def build_one_hot(j, carry):
        at = pl.ds(pl.multiple_of(j * 512, 512), 512)
        left = (antenna_id == pairs_ref[0:1, at]).astype(F32).astype(BF16)
        left_twice[:LANES, at] = left
        left_twice[LANES:, at] = left
        one_right[:, at] = (antenna_id == pairs_ref[1:2, at]).astype(F32).astype(BF16)
        return carry

    lax.fori_loop(0, nb // 512, build_one_hot, 0)
    inputs[8].wait()

    @pl.when(q == centre)
    def _():
        piece = min(64, 2 * nch)

        def split_tables(j, carry):
            at = pl.ds(pl.multiple_of(j * piece, piece), piece)
            for i in range(2):
                tables_hi[i, at, :], tables_lo[i, at, :] = split(tables[i, at, :])
            return carry

        lax.fori_loop(0, 2 * nch // piece, split_tables, 0)

    @pl.when(q == centre)
    def _():
        pl.semaphore_wait(barrier, nch - 1)

    @pl.when(q != centre)
    def _():
        pl.semaphore_wait(barrier, 2 * (ns - 1) + nf - 1)


    def send_sources(step, carry):
        j = quad_at(s // 4, step, quads)
        for i in range(4):
            peer = j * 4 + i

            @pl.when(peer != s)
            def _():
                pltpu.make_async_remote_copy(
                    src_ref=source_send.at[peer], dst_ref=source_recv.at[s], send_sem=send1,
                    recv_sem=recv1.at[s // 4], device_id={"src": peer}, device_id_type=MESH,
                ).start()

        return carry

    lax.fori_loop(0, quads, send_sources, 0)

    @pl.when(q == centre)
    def _():
        dat_recv[q] = data_ref[...]

    @pl.when(q != centre)
    def _():
        pltpu.make_async_remote_copy(
            src_ref=data_ref, dst_ref=dat_recv.at[q], send_sem=send2, recv_sem=recv2.at[q],
            device_id={"freq": centre}, device_id_type=MESH,
        ).start()

    def forward(step, carry):
        j = quad_at(s // 4, step, quads)

        @pl.when(step == 0)
        def _():
            at = pl.ds(0, 3)
            pltpu.make_async_copy(source_send.at[at], source_recv.at[at], recv1.at[j]).wait()

        @pl.when(step != 0)
        def _():
            at = pl.ds(0, 4)
            pltpu.make_async_copy(source_send.at[at], source_recv.at[at], recv1.at[j]).wait()

        expand(j * 4, even_hi, even_lo)
        correlate(odd_hi, odd_lo)
        expand(j * 4 + 1, odd_hi, odd_lo)
        correlate(even_hi, even_lo)
        expand(j * 4 + 2, even_hi, even_lo)
        correlate(odd_hi, odd_lo)
        expand(j * 4 + 3, odd_hi, odd_lo)
        correlate(even_hi, even_lo)
        return carry

    lax.fori_loop(0, quads, forward, 0)
    correlate(odd_hi, odd_lo)

    gram = gram_hh[...] + 2.0 * gram_hl[...]
    even = gram[:LANES, :LANES] + gram[LANES:, LANES:]
    odd = gram[LANES:, :LANES] - gram[:LANES, LANES:]
    vis_re = 0.5 * (even + even.T)
    vis_im = 0.5 * (odd - odd.T)
    grid_hi, grid_lo = split(jnp.concatenate([vis_re, -vis_im], axis=0))
    grid_parts = jnp.concatenate([grid_hi, grid_lo], axis=1)

    pair = min(2, quads)

    def gather(step, carry):
        chosen = [quad_at(s // 4, quads - 1 - step * pair - i, quads) for i in range(pair)]
        rows = []
        for j in chosen:
            at = pl.ds(pl.multiple_of(j * 512, 512), 512)
            picked = dot(grid_parts, left_twice[:, at])
            right = one_right[:, at].astype(F32)
            rows.append([
                jnp.sum(picked[c * LANES : (c + 1) * LANES] * right, axis=0, keepdims=True) for c in range(2)
            ])
        for j, row in zip(chosen, rows):
            for i in range(4):
                for c in range(2):
                    vis_send[j * 4 + i, c : c + 1, :] = row[c][:, i * LANES : (i + 1) * LANES]
        for j in chosen:
            for i in range(4):
                peer = j * 4 + i

                @pl.when(jnp.logical_or(peer != s, q != centre))
                def _():
                    pltpu.make_async_remote_copy(
                        src_ref=vis_send.at[peer], dst_ref=vis_all.at[q * ns + s], send_sem=send3, recv_sem=recv3,
                        device_id={"src": peer, "freq": centre}, device_id_type=MESH,
                    ).start()

        return carry

    lax.fori_loop(0, quads // pair, gather, 0)

    def add_parts(k, carry):
        for top in range(0, 2 * LANES, 64):
            at = pl.ds(top, 64)
            phased_sum[k, at, :] = phased_hi[k, at, :].astype(F32) + 2.0 * phased_lo[k, at, :].astype(F32)
        return carry

    lax.fori_loop(0, ns, add_parts, 0)
    most = pl.ds(0, ns - 1)
    others = pl.ds(0, nf - 1)
    all_but_one = pl.ds(0, nch - 1)

    @pl.when(q == centre)
    def _():
        def take_data(step, carry):
            other = lax.rem(q + step, nf)
            pltpu.make_async_remote_copy(
                src_ref=data_ref, dst_ref=dat_recv.at[other], send_sem=send2, recv_sem=recv2.at[other],
                device_id={"freq": other}, device_id_type=MESH,
            ).wait_recv()
            return carry

        lax.fori_loop(1, nf, take_data, 0)

        def three_passes(i, high, low):
            both = dot(tables_hi[i], jnp.concatenate([high, low], axis=1))
            return both[:, :LANES] + both[:, LANES:] + dot(tables_lo[i], high)

        weight = jnp.transpose(jnp.broadcast_to(dw_ref[...], (LANES, nch)))
        spectra = [
            jnp.transpose(jnp.concatenate([dat_recv[i, c] for i in range(nf)], axis=0)) for c in range(2)
        ]
        vis_all[q * ns + s] = vis_send[s]
        pltpu.make_async_copy(vis_all.at[all_but_one], vis_all.at[all_but_one], recv3).wait()

        def pack(j, carry):
            at = pl.ds(pl.multiple_of(j * 16, 16), 16)
            vis_rows[at, :] = jnp.concatenate([vis_all[j * 8 + i] for i in range(8)], axis=0)
            return carry

        lax.fori_loop(0, nch // 8, pack, 0)
        vis_hi, vis_lo = split(vis_rows[...])
        spec = three_passes(0, vis_hi, vis_lo)
        spec_cot = jnp.concatenate(
            [weight * (spec[:nch] - spectra[0]), weight * (spec[nch:] - spectra[1])], axis=0
        )
        cot_hi, cot_lo = split(spec_cot)
        vis_rows[...] = three_passes(1, cot_hi, cot_lo)

        def send_cot(step, carry):
            j = quad_at(s // 4, quads - 1 - step, quads)
            for group in range(nf):
                first = group * ns + j * 4
                piece = vis_rows[pl.ds(pl.multiple_of(first * 2, 8), 8), :]
                for i in range(4):
                    peer = j * 4 + i
                    cot_all[first + i] = piece[2 * i : 2 * i + 2]

                    def send():
                        pltpu.make_async_remote_copy(
                            src_ref=cot_all.at[first + i], dst_ref=cot_recv.at[s], send_sem=send6,
                            recv_sem=recv6.at[s // 4], device_id={"src": peer, "freq": group},
                            device_id_type=MESH,
                        ).start()

                    if group == centre:
                        pl.when(peer != s)(send)
                    else:
                        send()
            return carry

        lax.fori_loop(0, quads, send_cot, 0)
        cot_recv[s] = cot_all[q * ns + s]

    many = min(4, quads)

    def scatter(half, carry):
        total = grids_ref[...]
        for i in range(many):
            step = half * many + i
            j = quad_at(s // 4, step, quads)
            with_own = jnp.logical_and(step == 0, q == centre)

            @pl.when(with_own)
            def _():
                pltpu.make_async_copy(cot_recv.at[pl.ds(0, 3)], cot_recv.at[pl.ds(0, 3)], recv6.at[j]).wait()

            @pl.when(jnp.logical_not(with_own))
            def _():
                pltpu.make_async_copy(cot_recv.at[pl.ds(0, 4)], cot_recv.at[pl.ds(0, 4)], recv6.at[j]).wait()

        for i in range(many):
            j = quad_at(s // 4, half * many + i, quads)
            at = pl.ds(pl.multiple_of(j * 512, 512), 512)
            right = one_right[:, at]
            parts = []
            for c in range(2):
                row = jnp.concatenate([cot_recv[j * 4 + i, c : c + 1, :] for i in range(4)], axis=1)
                parts.append(split(row))
            scaled = [right * parts[c][part] for part in range(2) for c in range(2)]
            total = total + dot(left_twice[:LANES, at], jnp.concatenate(scaled, axis=0), NT)
        grids_ref[...] = total
        return carry

    grids_ref[...] = jnp.zeros_like(grids_ref)
    lax.fori_loop(0, quads // many, scatter, 0)
    grids = grids_ref[...]
    grids = grids[:, : 2 * LANES] + grids[:, 2 * LANES :]
    real, imag = grids[:, :LANES], grids[:, LANES:]
    real, imag = 0.5 * (real + real.T), 0.5 * (imag - imag.T)
    matrix = jnp.concatenate(
        [jnp.concatenate([real, -imag], axis=1), jnp.concatenate([imag, real], axis=1)], axis=0
    )
    matrix_parts = jnp.concatenate(split(matrix), axis=0)

    def pull_back(k):
        for lane in range(0, slots, 256):
            at = pl.ds(lane, 256)
            high = phased_hi[k, :, at]
            product = dot(matrix_parts, high)
            product = product[: 2 * LANES] + product[2 * LANES :]
            u_send[k, :, at] = jnp.sum(phased_sum[k, :, at] * product, axis=0, keepdims=True)

    def send_gradient(peer):
        pltpu.make_async_remote_copy(
            src_ref=u_send.at[peer], dst_ref=u_recv.at[s], send_sem=send7, recv_sem=recv7,
            device_id={"src": peer}, device_id_type=MESH,
        ).start()

    def backward(step, carry):
        j = quad_at(s // 4, quads - 1 - step, quads)
        for i in range(4):
            pull_back(j * 4 + i)
        for i in range(4):
            send_gradient(j * 4 + i)
        return carry

    lax.fori_loop(0, quads - 1, backward, 0)
    for step in (2, 1, 3):
        pull_back(in_quad(s, step))
    for step in (2, 1, 3):
        send_gradient(in_quad(s, step))
    pull_back(s)
    u_recv[s] = u_send[s]
    pltpu.make_async_copy(u_send.at[most], u_recv.at[most], recv7).wait()
    for i in range(ns):
        u_ref[i : i + 1, :] = u_recv[i]
    flux_send[0] = jnp.sum(u_ref[...], axis=0, keepdims=True)

    def send_flux(step, carry):
        other = lax.rem(q + step, nf)
        pltpu.make_async_remote_copy(
            src_ref=flux_send, dst_ref=flux_recv.at[pl.ds(q, 1)], send_sem=send8, recv_sem=recv8,
            device_id={"freq": other}, device_id_type=MESH,
        ).start()
        return carry

    lax.fori_loop(1, nf, send_flux, 0)
    flux_recv[q] = flux_send[0]
    pltpu.make_async_copy(source_send.at[most], source_recv.at[most], send1).wait()
    pltpu.make_async_copy(u_send.at[most], u_recv.at[most], send7).wait()

    @pl.when(q == centre)
    def _():
        pltpu.make_async_copy(vis_send.at[most], vis_send.at[most], send3).wait()
        pltpu.make_async_copy(cot_all.at[all_but_one], cot_all.at[all_but_one], send6).wait()

    @pl.when(q != centre)
    def _():
        pltpu.make_async_copy(vis_send, vis_send, send3).wait()
        pltpu.make_async_copy(data_ref, dat_recv.at[0], send2).wait()

    pltpu.make_async_copy(flux_recv.at[others], flux_recv.at[others], recv8).wait()
    total = flux_recv[0]
    for i in range(1, nf):
        total = total + flux_recv[i]
    total_ref[...] = total
    pltpu.make_async_copy(flux_recv.at[others], flux_recv.at[others], send8).wait()


def body(source_dirs, flux, beam, counts, antennas, pairs, data, delay_weight):
    ns, nf = lax.axis_size("src"), lax.axis_size("freq")
    slots = flux.shape[0]
    nch = ns * nf
    share = LANES // nf
    vmem, hbm = pl.BlockSpec(memory_space=pltpu.VMEM), pl.BlockSpec(memory_space=pltpu.HBM)
    dma = pltpu.SemaphoreType.DMA
    macs = 4 * ns * slots * 256 * 256
    tables = jnp.asarray(delay_tables(nch))
    inputs = (
        source_dirs, flux[None, :], beam, counts, antennas, pairs, jnp.transpose(data, (0, 2, 1)),
        delay_weight[None, :], tables,
    )
    gradient, total = pl.pallas_call(
        functools.partial(kernel, ns, nf, min(3, nf - 1)),
        out_shape=(
            pltpu.VMEM((ns, slots), F32),
            pltpu.VMEM((1, slots), F32),
        ),
        in_specs=[hbm] * len(inputs),
        out_specs=(vmem, vmem),
        scratch_shapes=[
            (pltpu.SMEM if i == 3 else pltpu.VMEM)(value.shape, value.dtype) for i, value in enumerate(inputs)
        ] + [
            pltpu.VMEM((ns, 12, LANES), F32),
            pltpu.VMEM((ns, 12, LANES), F32),
            pltpu.VMEM((ns, 2 * LANES, slots), BF16),
            pltpu.VMEM((ns, 2 * LANES, slots), BF16),
            pltpu.VMEM((ns, 2 * LANES, slots), F32),
            pltpu.VMEM((2 * LANES, ns * LANES), BF16),
            pltpu.VMEM((LANES, ns * LANES), BF16),
            pltpu.VMEM((4 * LANES, LANES), BF16),
            pltpu.VMEM((2 * LANES, slots), BF16),
            pltpu.VMEM((2 * LANES, slots), BF16),
            pltpu.VMEM((2 * LANES, slots), BF16),
            pltpu.VMEM((2 * LANES, slots), BF16),
            pltpu.VMEM((2 * LANES, 2 * LANES), F32),
            pltpu.VMEM((2 * LANES, 2 * LANES), F32),
            pltpu.VMEM((LANES, 4 * LANES), F32),
            pltpu.VMEM((ns, 2, LANES), F32),
            pltpu.VMEM((nch, 2, LANES), F32),
            pltpu.VMEM((2 * nch, LANES), F32),
            pltpu.VMEM((nf, 2, share, nch), F32),
            pltpu.VMEM((2, 2 * nch, 2 * nch), BF16),
            pltpu.VMEM((2, 2 * nch, 2 * nch), BF16),
            pltpu.VMEM((nch, 2, LANES), F32),
            pltpu.VMEM((ns, 2, LANES), F32),
            pltpu.VMEM((ns, 1, slots), F32),
            pltpu.VMEM((ns, 1, slots), F32),
            pltpu.VMEM((1, 1, slots), F32),
            pltpu.VMEM((nf, 1, slots), F32),
            dma((len(inputs),)),
            dma, dma((ns // 4,)),
            dma, dma((nf,)),
            dma, dma,
            dma, dma((ns // 4,)),
            dma, dma,
            dma, dma,
        ],
        compiler_params=pltpu.CompilerParams(
            collective_id=0, has_side_effects=True, vmem_limit_bytes=63 * 1024 * 1024
        ),
        cost_estimate=pl.CostEstimate(flops=2 * macs, bytes_accessed=4 * 1024 * 1024, transcendentals=0),
    )(*inputs)
    return (total[0] / flux, 2.0 * gradient / beam)


def solution(mesh):
    in_specs = (
        P(None, "src"),
        P("src"),
        P("freq", "src"),
        P(),
        P(),
        P(),
        P(None, None, ("src", "freq")),
        P(),
    )
    out_specs = (P("src"), P("freq", "src"))
    return jax.shard_map(body, mesh=mesh, in_specs=in_specs, out_specs=out_specs, check_vma=False)
```

```python
import functools
import math

import jax
import jax.numpy as jnp
import numpy as np
from jax import lax
from jax.experimental import pallas as pl
from jax.experimental.pallas import tpu as pltpu
from jax.sharding import PartitionSpec as P

TWO_PI = 2.0 * math.pi
MESH = pl.DeviceIdType.MESH
F32 = jnp.float32
BF16 = jnp.bfloat16
LANES = 128
NT = (((1,), (1,)), ((), ()))
NN = (((1,), (0,)), ((), ()))
SIN_POLY = (3.1415902702069913, -5.167406733272317, 2.544010518503151, -0.5594624554674011)
COS_POLY = (0.9999932488527381, -4.933934668076284, 4.041248101995494, -1.2220317625317256)


def dot(left, right, dims=NN):
    return lax.dot_general(left, right, dims, preferred_element_type=F32)


def split(value):
    high = value.astype(BF16)
    return high, (value - high.astype(F32)).astype(BF16)


def horner(coefficients, variable):
    total = coefficients[-1] * variable + coefficients[-2]
    for coefficient in coefficients[-3::-1]:
        total = total * variable + coefficient
    return total


def scaled_cos_sin(turns, root):
    rest = turns - jnp.round(turns)
    square = rest * rest
    sine = rest * horner(SIN_POLY, square)
    twice = (2.0 * root) * sine
    return root - twice * sine, twice * horner(COS_POLY, square)


def three_parts(value):
    first = value.astype(BF16).astype(F32)
    rest = value - first
    second = rest.astype(BF16).astype(F32)
    return first, second, (rest - second).astype(BF16).astype(F32)


def delay_tables(nch):
    index = np.arange(nch)
    angle = 2.0 * np.pi * ((index[:, None] * index[None, :]) % nch) / nch
    taper = 0.6 - 0.4 * np.cos(2.0 * np.pi * (index + 0.5) / nch)
    cos, sin = np.cos(angle) / math.sqrt(nch), np.sin(angle) / math.sqrt(nch)
    forward = np.zeros((2, nch, nch, 2))
    forward[0, :, :, 0] = cos
    forward[0, :, :, 1] = sin
    forward[1, :, :, 0] = -sin
    forward[1, :, :, 1] = cos
    forward *= taper[None, None, :, None]
    forward = forward.reshape(2 * nch, 2 * nch)
    return np.stack([forward, forward.T]).astype(np.float32)


def in_quad(own, step):
    return own // 4 * 4 + lax.rem(own + step, 4)


def quad_at(own, step, count):
    if count != 8:
        return lax.rem(own + step, count)
    place = lax.rem(step, 4)
    y = lax.rem(own // 2 + place + place // 2 * (5 - 2 * place), 4)
    z = lax.rem(lax.rem(own, 2) + step // 4, 2)
    return y * 2 + z


def kernel(
    ns, nf, centre,
    dirs_hbm, flux_hbm, beam_hbm, counts_hbm, ant_hbm, pairs_hbm, data_hbm, dw_hbm, tables_hbm,
    u_ref, total_ref,
    dirs_ref, flux_ref, beam_ref, counts_ref, ant_ref, pairs_ref, data_ref, dw_ref, tables,
    source_send, source_recv, phased_hi, phased_lo, phased_sum, left_twice, one_right, ant_parts, even_hi, even_lo, odd_hi, odd_lo, gram_hh, gram_hl, grids_ref,
    vis_send, vis_all, vis_rows, dat_recv, tables_hi, tables_lo, cot_all, cot_recv,
    u_send, u_recv, flux_send, flux_recv,
    input_sem, send1, recv1, send2, recv2, send3, recv3, send6, recv6, send7, recv7,
    send8, recv8,
):
    nch = ns * nf
    slots = dirs_ref.shape[1]
    nb = ns * LANES
    quads = ns // 4
    s = lax.axis_index("src")
    q = lax.axis_index("freq")

    inputs = [
        pltpu.make_async_copy(hbm, vmem, input_sem.at[i])
        for i, (hbm, vmem) in enumerate((
            (dirs_hbm, dirs_ref), (flux_hbm, flux_ref), (beam_hbm, beam_ref), (counts_hbm, counts_ref),
            (ant_hbm, ant_ref), (pairs_hbm, pairs_ref), (data_hbm, data_ref), (dw_hbm, dw_ref),
            (tables_hbm, tables),
        ))
    ]
    barrier = pltpu.get_barrier_semaphore()

    def greet(peer, group):
        pl.semaphore_signal(barrier, inc=1, device_id={"src": peer, "freq": group}, device_id_type=MESH)

    def greet_quad(step, carry):
        j = quad_at(s // 4, quads - 1 - step, quads)
        for i in range(4):
            peer = j * 4 + i

            @pl.when(peer != s)
            def _():
                greet(peer, q)

                @pl.when(q != centre)
                def _():
                    greet(peer, centre)

                @pl.when(q == centre)
                def _():
                    for group in range(nf):
                        if group != centre:
                            greet(peer, group)

        return carry

    def greet_freq(step, carry):
        greet(s, lax.rem(q + step, nf))
        return carry

    lax.fori_loop(0, quads, greet_quad, 0)
    lax.fori_loop(1, nf, greet_freq, 0)
    for copy in inputs:
        copy.start()
    for copy in inputs[:8]:
        copy.wait()

    live = lax.broadcasted_iota(jnp.int32, (1, slots), 1) < counts_ref[s]
    strength = jnp.where(live, jnp.sqrt(flux_ref[...] * (1.0 / math.sqrt(slots * ns))), 0.0)
    roots = beam_ref[...] * strength
    along = jnp.concatenate(
        [dirs_ref[i : i + 1, pl.ds(j * LANES, LANES)] for i in range(2) for j in range(4)], axis=0
    )
    for i in range(ns):
        source_send[i, 0:8, :] = along
        for j in range(4):
            source_send[i, 8 + j : 9 + j, :] = roots[i : i + 1, j * LANES : (j + 1) * LANES]
    source_recv[s] = source_send[s]

    freq = 1.0 + 0.6 * (q * ns + s).astype(F32) / nch
    positions = jnp.concatenate(
        [jnp.broadcast_to(ant_ref[i : i + 1, :] * freq, (4, LANES)) for i in range(3)]
        + [jnp.zeros((4, LANES), F32)],
        axis=0,
    )
    row = lax.broadcasted_iota(jnp.int32, (16, LANES), 0)
    for j in range(4):
        first, second, third = three_parts(jnp.where(row % 4 == j, positions, 0.0))
        spare = jnp.zeros((LANES - 96, LANES), F32)
        ant_parts[j * LANES : (j + 1) * LANES, :] = jnp.transpose(
            jnp.concatenate([first, second, third, first, second, first, spare], axis=0)
        ).astype(BF16)

    gram_hh[...] = jnp.zeros_like(gram_hh)
    gram_hl[...] = jnp.zeros_like(gram_hl)

    def expand(k, high_ref, low_ref):
        source = source_recv[k]
        along_l, along_m = source[0:4], source[4:8]
        along_n = jnp.sqrt(1.0 - along_l * along_l - along_m * along_m)
        source = jnp.concatenate([along_l, along_m, along_n, jnp.zeros_like(along_n)], axis=0)
        first, second, third = three_parts(source)
        parts = jnp.concatenate([first, first, first, second, second, third], axis=0).astype(BF16)
        turns = dot(ant_parts[:, :96], parts)
        for lane in range(0, slots, LANES):
            piece = lane // LANES
            root = source_recv[k, 8 + piece : 9 + piece, :]
            for top in range(0, LANES, 64):
                cosine, sine = scaled_cos_sin(turns[lane + top : lane + top + 64], root)
                for base, value in ((0, cosine), (LANES, sine)):
                    high, low = split(value)
                    at = (pl.ds(base + top, 64), pl.ds(lane, LANES))
                    phased_hi[(k, *at)] = high
                    phased_lo[(k, *at)] = low
                    high_ref[at] = high
                    low_ref[at] = low

    def correlate(high_ref, low_ref):
        high = high_ref[...]
        gram_hh[...] += dot(high, high, NT)
        gram_hl[...] += dot(high, low_ref[...], NT)

    odd_hi[...] = jnp.zeros_like(odd_hi)
    odd_lo[...] = jnp.zeros_like(odd_lo)

    antenna_id = lax.broadcasted_iota(jnp.int32, (LANES, 512), 0)

    def build_one_hot(j, carry):
        at = pl.ds(pl.multiple_of(j * 512, 512), 512)
        left = (antenna_id == pairs_ref[0:1, at]).astype(F32).astype(BF16)
        left_twice[:LANES, at] = left
        left_twice[LANES:, at] = left
        one_right[:, at] = (antenna_id == pairs_ref[1:2, at]).astype(F32).astype(BF16)
        return carry

    lax.fori_loop(0, nb // 512, build_one_hot, 0)
    inputs[8].wait()

    @pl.when(q == centre)
    def _():
        piece = min(64, 2 * nch)

        def split_tables(j, carry):
            at = pl.ds(pl.multiple_of(j * piece, piece), piece)
            for i in range(2):
                tables_hi[i, at, :], tables_lo[i, at, :] = split(tables[i, at, :])
            return carry

        lax.fori_loop(0, 2 * nch // piece, split_tables, 0)

    @pl.when(q == centre)
    def _():
        pl.semaphore_wait(barrier, nch - 1)

    @pl.when(q != centre)
    def _():
        pl.semaphore_wait(barrier, 2 * (ns - 1) + nf - 1)


    def send_sources(step, carry):
        j = quad_at(s // 4, step, quads)
        for i in range(4):
            peer = j * 4 + i

            @pl.when(peer != s)
            def _():
                pltpu.make_async_remote_copy(
                    src_ref=source_send.at[peer], dst_ref=source_recv.at[s], send_sem=send1,
                    recv_sem=recv1.at[s // 4], device_id={"src": peer}, device_id_type=MESH,
                ).start()

        return carry

    lax.fori_loop(0, quads, send_sources, 0)

    @pl.when(q == centre)
    def _():
        dat_recv[q] = data_ref[...]

    @pl.when(q != centre)
    def _():
        pltpu.make_async_remote_copy(
            src_ref=data_ref, dst_ref=dat_recv.at[q], send_sem=send2, recv_sem=recv2.at[q],
            device_id={"freq": centre}, device_id_type=MESH,
        ).start()

    def forward(step, carry):
        j = quad_at(s // 4, step, quads)

        @pl.when(step == 0)
        def _():
            at = pl.ds(0, 3)
            pltpu.make_async_copy(source_send.at[at], source_recv.at[at], recv1.at[j]).wait()

        @pl.when(step != 0)
        def _():
            at = pl.ds(0, 4)
            pltpu.make_async_copy(source_send.at[at], source_recv.at[at], recv1.at[j]).wait()

        expand(j * 4, even_hi, even_lo)
        correlate(odd_hi, odd_lo)
        expand(j * 4 + 1, odd_hi, odd_lo)
        correlate(even_hi, even_lo)
        expand(j * 4 + 2, even_hi, even_lo)
        correlate(odd_hi, odd_lo)
        expand(j * 4 + 3, odd_hi, odd_lo)
        correlate(even_hi, even_lo)
        return carry

    lax.fori_loop(0, quads, forward, 0)
    correlate(odd_hi, odd_lo)

    gram = gram_hh[...] + 2.0 * gram_hl[...]
    even = gram[:LANES, :LANES] + gram[LANES:, LANES:]
    odd = gram[LANES:, :LANES] - gram[:LANES, LANES:]
    vis_re = 0.5 * (even + even.T)
    vis_im = 0.5 * (odd - odd.T)
    grid_hi, grid_lo = split(jnp.concatenate([vis_re, -vis_im], axis=0))
    grid_parts = jnp.concatenate([grid_hi, grid_lo], axis=1)

    pair = min(2, quads)

    def gather(step, carry):
        chosen = [quad_at(s // 4, quads - 1 - step * pair - i, quads) for i in range(pair)]
        rows = []
        for j in chosen:
            at = pl.ds(pl.multiple_of(j * 512, 512), 512)
            picked = dot(grid_parts, left_twice[:, at])
            right = one_right[:, at].astype(F32)
            rows.append([
                jnp.sum(picked[c * LANES : (c + 1) * LANES] * right, axis=0, keepdims=True) for c in range(2)
            ])
        for j, row in zip(chosen, rows):
            for i in range(4):
                for c in range(2):
                    vis_send[j * 4 + i, c : c + 1, :] = row[c][:, i * LANES : (i + 1) * LANES]
        for j in chosen:
            for i in range(4):
                peer = j * 4 + i

                @pl.when(jnp.logical_or(peer != s, q != centre))
                def _():
                    pltpu.make_async_remote_copy(
                        src_ref=vis_send.at[peer], dst_ref=vis_all.at[q * ns + s], send_sem=send3, recv_sem=recv3,
                        device_id={"src": peer, "freq": centre}, device_id_type=MESH,
                    ).start()

        return carry

    lax.fori_loop(0, quads // pair, gather, 0)

    def add_parts(k, carry):
        for top in range(0, 2 * LANES, 64):
            at = pl.ds(top, 64)
            phased_sum[k, at, :] = phased_hi[k, at, :].astype(F32) + 2.0 * phased_lo[k, at, :].astype(F32)
        return carry

    lax.fori_loop(0, ns, add_parts, 0)
    most = pl.ds(0, ns - 1)
    others = pl.ds(0, nf - 1)
    all_but_one = pl.ds(0, nch - 1)

    @pl.when(q == centre)
    def _():
        def take_data(step, carry):
            other = lax.rem(q + step, nf)
            pltpu.make_async_remote_copy(
                src_ref=data_ref, dst_ref=dat_recv.at[other], send_sem=send2, recv_sem=recv2.at[other],
                device_id={"freq": other}, device_id_type=MESH,
            ).wait_recv()
            return carry

        lax.fori_loop(1, nf, take_data, 0)

        def three_passes(i, high, low):
            both = dot(tables_hi[i], jnp.concatenate([high, low], axis=1))
            return both[:, :LANES] + both[:, LANES:] + dot(tables_lo[i], high)

        weight = jnp.transpose(jnp.broadcast_to(dw_ref[...], (LANES, nch)))
        spectra = [
            jnp.transpose(jnp.concatenate([dat_recv[i, c] for i in range(nf)], axis=0)) for c in range(2)
        ]
        vis_all[q * ns + s] = vis_send[s]
        pltpu.make_async_copy(vis_all.at[all_but_one], vis_all.at[all_but_one], recv3).wait()

        def pack(j, carry):
            at = pl.ds(pl.multiple_of(j * 16, 16), 16)
            vis_rows[at, :] = jnp.concatenate([vis_all[j * 8 + i] for i in range(8)], axis=0)
            return carry

        lax.fori_loop(0, nch // 8, pack, 0)
        vis_hi, vis_lo = split(vis_rows[...])
        spec = three_passes(0, vis_hi, vis_lo)
        spec_cot = jnp.concatenate(
            [weight * (spec[:nch] - spectra[0]), weight * (spec[nch:] - spectra[1])], axis=0
        )
        cot_hi, cot_lo = split(spec_cot)
        vis_rows[...] = three_passes(1, cot_hi, cot_lo)

        def send_cot(step, carry):
            j = quad_at(s // 4, quads - 1 - step, quads)
            for group in range(nf):
                first = group * ns + j * 4
                piece = vis_rows[pl.ds(pl.multiple_of(first * 2, 8), 8), :]
                for i in range(4):
                    peer = j * 4 + i
                    cot_all[first + i] = piece[2 * i : 2 * i + 2]

                    def send():
                        pltpu.make_async_remote_copy(
                            src_ref=cot_all.at[first + i], dst_ref=cot_recv.at[s], send_sem=send6,
                            recv_sem=recv6.at[s // 4], device_id={"src": peer, "freq": group},
                            device_id_type=MESH,
                        ).start()

                    if group == centre:
                        pl.when(peer != s)(send)
                    else:
                        send()
            return carry

        lax.fori_loop(0, quads, send_cot, 0)
        cot_recv[s] = cot_all[q * ns + s]

    many = min(4, quads)

    def scatter(half, carry):
        total = grids_ref[...]
        for i in range(many):
            step = half * many + i
            j = quad_at(s // 4, step, quads)
            with_own = jnp.logical_and(step == 0, q == centre)

            @pl.when(with_own)
            def _():
                pltpu.make_async_copy(cot_recv.at[pl.ds(0, 3)], cot_recv.at[pl.ds(0, 3)], recv6.at[j]).wait()

            @pl.when(jnp.logical_not(with_own))
            def _():
                pltpu.make_async_copy(cot_recv.at[pl.ds(0, 4)], cot_recv.at[pl.ds(0, 4)], recv6.at[j]).wait()

        for i in range(many):
            j = quad_at(s // 4, half * many + i, quads)
            at = pl.ds(pl.multiple_of(j * 512, 512), 512)
            right = one_right[:, at]
            parts = []
            for c in range(2):
                row = jnp.concatenate([cot_recv[j * 4 + i, c : c + 1, :] for i in range(4)], axis=1)
                parts.append(split(row))
            scaled = [right * parts[c][part] for part in range(2) for c in range(2)]
            total = total + dot(left_twice[:LANES, at], jnp.concatenate(scaled, axis=0), NT)
        grids_ref[...] = total
        return carry

    grids_ref[...] = jnp.zeros_like(grids_ref)
    lax.fori_loop(0, quads // many, scatter, 0)
    grids = grids_ref[...]
    grids = grids[:, : 2 * LANES] + grids[:, 2 * LANES :]
    real, imag = grids[:, :LANES], grids[:, LANES:]
    real, imag = 0.5 * (real + real.T), 0.5 * (imag - imag.T)
    matrix = jnp.concatenate(
        [jnp.concatenate([real, -imag], axis=1), jnp.concatenate([imag, real], axis=1)], axis=0
    )
    matrix_parts = jnp.concatenate(split(matrix), axis=0)

    def pull_back(k):
        for lane in range(0, slots, 256):
            at = pl.ds(lane, 256)
            high = phased_hi[k, :, at]
            product = dot(matrix_parts, high)
            product = product[: 2 * LANES] + product[2 * LANES :]
            u_send[k, :, at] = jnp.sum(phased_sum[k, :, at] * product, axis=0, keepdims=True)

    def send_gradient(peer):
        pltpu.make_async_remote_copy(
            src_ref=u_send.at[peer], dst_ref=u_recv.at[s], send_sem=send7, recv_sem=recv7,
            device_id={"src": peer}, device_id_type=MESH,
        ).start()

    def backward(step, carry):
        j = quad_at(s // 4, quads - 1 - step, quads)
        for i in range(4):
            pull_back(j * 4 + i)
        for i in range(4):
            send_gradient(j * 4 + i)
        return carry

    lax.fori_loop(0, quads - 1, backward, 0)
    for step in (2, 1, 3):
        pull_back(in_quad(s, step))
    for step in (2, 1, 3):
        send_gradient(in_quad(s, step))
    pull_back(s)
    u_recv[s] = u_send[s]
    pltpu.make_async_copy(u_send.at[most], u_recv.at[most], recv7).wait()
    for i in range(ns):
        u_ref[i : i + 1, :] = u_recv[i]
    flux_send[0] = jnp.sum(u_ref[...], axis=0, keepdims=True)

    def send_flux(step, carry):
        other = lax.rem(q + step, nf)
        pltpu.make_async_remote_copy(
            src_ref=flux_send, dst_ref=flux_recv.at[pl.ds(q, 1)], send_sem=send8, recv_sem=recv8,
            device_id={"freq": other}, device_id_type=MESH,
        ).start()
        return carry

    lax.fori_loop(1, nf, send_flux, 0)
    flux_recv[q] = flux_send[0]
    pltpu.make_async_copy(source_send.at[most], source_recv.at[most], send1).wait()
    pltpu.make_async_copy(u_send.at[most], u_recv.at[most], send7).wait()

    @pl.when(q == centre)
    def _():
        pltpu.make_async_copy(vis_send.at[most], vis_send.at[most], send3).wait()
        pltpu.make_async_copy(cot_all.at[all_but_one], cot_all.at[all_but_one], send6).wait()

    @pl.when(q != centre)
    def _():
        pltpu.make_async_copy(vis_send, vis_send, send3).wait()
        pltpu.make_async_copy(data_ref, dat_recv.at[0], send2).wait()

    pltpu.make_async_copy(flux_recv.at[others], flux_recv.at[others], recv8).wait()
    total = flux_recv[0]
    for i in range(1, nf):
        total = total + flux_recv[i]
    total_ref[...] = total
    pltpu.make_async_copy(flux_recv.at[others], flux_recv.at[others], send8).wait()


def body(source_dirs, flux, beam, counts, antennas, pairs, data, delay_weight):
    ns, nf = lax.axis_size("src"), lax.axis_size("freq")
    slots = flux.shape[0]
    nch = ns * nf
    share = LANES // nf
    vmem, hbm = pl.BlockSpec(memory_space=pltpu.VMEM), pl.BlockSpec(memory_space=pltpu.HBM)
    dma = pltpu.SemaphoreType.DMA
    macs = 4 * ns * slots * 256 * 256
    tables = jnp.asarray(delay_tables(nch))
    inputs = (
        source_dirs, flux[None, :], beam, counts, antennas, pairs, jnp.transpose(data, (0, 2, 1)),
        delay_weight[None, :], tables,
    )
    gradient, total = pl.pallas_call(
        functools.partial(kernel, ns, nf, min(3, nf - 1)),
        out_shape=(
            pltpu.VMEM((ns, slots), F32),
            pltpu.VMEM((1, slots), F32),
        ),
        in_specs=[hbm] * len(inputs),
        out_specs=(vmem, vmem),
        scratch_shapes=[
            (pltpu.SMEM if i == 3 else pltpu.VMEM)(value.shape, value.dtype) for i, value in enumerate(inputs)
        ] + [
            pltpu.VMEM((ns, 12, LANES), F32),
            pltpu.VMEM((ns, 12, LANES), F32),
            pltpu.VMEM((ns, 2 * LANES, slots), BF16),
            pltpu.VMEM((ns, 2 * LANES, slots), BF16),
            pltpu.VMEM((ns, 2 * LANES, slots), F32),
            pltpu.VMEM((2 * LANES, ns * LANES), BF16),
            pltpu.VMEM((LANES, ns * LANES), BF16),
            pltpu.VMEM((4 * LANES, LANES), BF16),
            pltpu.VMEM((2 * LANES, slots), BF16),
            pltpu.VMEM((2 * LANES, slots), BF16),
            pltpu.VMEM((2 * LANES, slots), BF16),
            pltpu.VMEM((2 * LANES, slots), BF16),
            pltpu.VMEM((2 * LANES, 2 * LANES), F32),
            pltpu.VMEM((2 * LANES, 2 * LANES), F32),
            pltpu.VMEM((LANES, 4 * LANES), F32),
            pltpu.VMEM((ns, 2, LANES), F32),
            pltpu.VMEM((nch, 2, LANES), F32),
            pltpu.VMEM((2 * nch, LANES), F32),
            pltpu.VMEM((nf, 2, share, nch), F32),
            pltpu.VMEM((2, 2 * nch, 2 * nch), BF16),
            pltpu.VMEM((2, 2 * nch, 2 * nch), BF16),
            pltpu.VMEM((nch, 2, LANES), F32),
            pltpu.VMEM((ns, 2, LANES), F32),
            pltpu.VMEM((ns, 1, slots), F32),
            pltpu.VMEM((ns, 1, slots), F32),
            pltpu.VMEM((1, 1, slots), F32),
            pltpu.VMEM((nf, 1, slots), F32),
            dma((len(inputs),)),
            dma, dma((ns // 4,)),
            dma, dma((nf,)),
            dma, dma,
            dma, dma((ns // 4,)),
            dma, dma,
            dma, dma,
        ],
        compiler_params=pltpu.CompilerParams(
            collective_id=0, has_side_effects=True, vmem_limit_bytes=63 * 1024 * 1024
        ),
        cost_estimate=pl.CostEstimate(flops=2 * macs, bytes_accessed=4 * 1024 * 1024, transcendentals=0),
    )(*inputs)
    return (total[0] / flux, 2.0 * gradient / beam)


def solution(mesh):
    in_specs = (
        P(None, "src"),
        P("src"),
        P("freq", "src"),
        P(),
        P(),
        P(),
        P(None, None, ("src", "freq")),
        P(),
    )
    out_specs = (P("src"), P("freq", "src"))
    return jax.shard_map(body, mesh=mesh, in_specs=in_specs, out_specs=out_specs, check_vma=False)
```

```python
import functools
import math

import jax
import jax.numpy as jnp
import numpy as np
from jax import lax
from jax.experimental import pallas as pl
from jax.experimental.pallas import tpu as pltpu
from jax.sharding import PartitionSpec as P

TWO_PI = 2.0 * math.pi
MESH = pl.DeviceIdType.MESH
F32 = jnp.float32
BF16 = jnp.bfloat16
LANES = 128
NT = (((1,), (1,)), ((), ()))
NN = (((1,), (0,)), ((), ()))
SIN_POLY = (3.1415902702069913, -5.167406733272317, 2.544010518503151, -0.5594624554674011)
COS_POLY = (0.9999932488527381, -4.933934668076284, 4.041248101995494, -1.2220317625317256)


def dot(left, right, dims=NN):
    return lax.dot_general(left, right, dims, preferred_element_type=F32)


def split(value):
    high = value.astype(BF16)
    return high, (value - high.astype(F32)).astype(BF16)


def horner(coefficients, variable):
    total = coefficients[-1] * variable + coefficients[-2]
    for coefficient in coefficients[-3::-1]:
        total = total * variable + coefficient
    return total


def scaled_cos_sin(turns, root):
    rest = turns - jnp.round(turns)
    square = rest * rest
    sine = rest * horner(SIN_POLY, square)
    twice = (2.0 * root) * sine
    return root - twice * sine, twice * horner(COS_POLY, square)


def three_parts(value):
    first = value.astype(BF16).astype(F32)
    rest = value - first
    second = rest.astype(BF16).astype(F32)
    return first, second, (rest - second).astype(BF16).astype(F32)


def delay_tables(nch):
    index = np.arange(nch)
    angle = 2.0 * np.pi * ((index[:, None] * index[None, :]) % nch) / nch
    taper = 0.6 - 0.4 * np.cos(2.0 * np.pi * (index + 0.5) / nch)
    cos, sin = np.cos(angle) / math.sqrt(nch), np.sin(angle) / math.sqrt(nch)
    forward = np.zeros((2, nch, nch, 2))
    forward[0, :, :, 0] = cos
    forward[0, :, :, 1] = sin
    forward[1, :, :, 0] = -sin
    forward[1, :, :, 1] = cos
    forward *= taper[None, None, :, None]
    forward = forward.reshape(2 * nch, 2 * nch)
    return np.stack([forward, forward.T]).astype(np.float32)


def in_quad(own, step):
    return own // 4 * 4 + lax.rem(own + step, 4)


def quad_at(own, step, count):
    if count != 8:
        return lax.rem(own + step, count)
    place = lax.rem(step, 4)
    y = lax.rem(own // 2 + place + place // 2 * (5 - 2 * place), 4)
    z = lax.rem(lax.rem(own, 2) + step // 4, 2)
    return y * 2 + z


def kernel(
    ns, nf, centre,
    dirs_hbm, flux_hbm, beam_hbm, counts_hbm, ant_hbm, pairs_hbm, data_hbm, dw_hbm, tables_hbm,
    u_ref, total_ref,
    dirs_ref, flux_ref, beam_ref, counts_ref, ant_ref, pairs_ref, data_ref, dw_ref, tables,
    source_send, source_recv, phased_hi, phased_lo, phased_sum, left_twice, one_right, ant_parts, even_hi, even_lo, odd_hi, odd_lo, gram_hh, gram_hl, grids_ref,
    vis_send, vis_all, vis_rows, dat_recv, tables_hi, tables_lo, cot_all, cot_recv,
    u_send, u_recv, flux_send, flux_recv,
    input_sem, send1, recv1, send2, recv2, send3, recv3, send6, recv6, send7, recv7,
    send8, recv8,
):
    nch = ns * nf
    slots = dirs_ref.shape[1]
    nb = ns * LANES
    quads = ns // 4
    s = lax.axis_index("src")
    q = lax.axis_index("freq")

    inputs = [
        pltpu.make_async_copy(hbm, vmem, input_sem.at[i])
        for i, (hbm, vmem) in enumerate((
            (dirs_hbm, dirs_ref), (flux_hbm, flux_ref), (beam_hbm, beam_ref), (counts_hbm, counts_ref),
            (ant_hbm, ant_ref), (pairs_hbm, pairs_ref), (data_hbm, data_ref), (dw_hbm, dw_ref),
            (tables_hbm, tables),
        ))
    ]
    barrier = pltpu.get_barrier_semaphore()

    def greet(peer, group):
        pl.semaphore_signal(barrier, inc=1, device_id={"src": peer, "freq": group}, device_id_type=MESH)

    def greet_quad(step, carry):
        j = quad_at(s // 4, quads - 1 - step, quads)
        for i in range(4):
            peer = j * 4 + i

            @pl.when(peer != s)
            def _():
                greet(peer, q)

                @pl.when(q != centre)
                def _():
                    greet(peer, centre)

                @pl.when(q == centre)
                def _():
                    for group in range(nf):
                        if group != centre:
                            greet(peer, group)

        return carry

    def greet_freq(step, carry):
        greet(s, lax.rem(q + step, nf))
        return carry

    lax.fori_loop(0, quads, greet_quad, 0)
    lax.fori_loop(1, nf, greet_freq, 0)
    for copy in inputs:
        copy.start()
    for copy in inputs[:8]:
        copy.wait()

    live = lax.broadcasted_iota(jnp.int32, (1, slots), 1) < counts_ref[s]
    strength = jnp.where(live, jnp.sqrt(flux_ref[...] * (1.0 / math.sqrt(slots * ns))), 0.0)
    roots = beam_ref[...] * strength
    along = jnp.concatenate(
        [dirs_ref[i : i + 1, pl.ds(j * LANES, LANES)] for i in range(2) for j in range(4)], axis=0
    )
    for i in range(ns):
        source_send[i, 0:8, :] = along
        for j in range(4):
            source_send[i, 8 + j : 9 + j, :] = roots[i : i + 1, j * LANES : (j + 1) * LANES]
    source_recv[s] = source_send[s]

    freq = 1.0 + 0.6 * (q * ns + s).astype(F32) / nch
    positions = jnp.concatenate(
        [jnp.broadcast_to(ant_ref[i : i + 1, :] * freq, (4, LANES)) for i in range(3)]
        + [jnp.zeros((4, LANES), F32)],
        axis=0,
    )
    row = lax.broadcasted_iota(jnp.int32, (16, LANES), 0)
    for j in range(4):
        first, second, third = three_parts(jnp.where(row % 4 == j, positions, 0.0))
        spare = jnp.zeros((LANES - 96, LANES), F32)
        ant_parts[j * LANES : (j + 1) * LANES, :] = jnp.transpose(
            jnp.concatenate([first, second, third, first, second, first, spare], axis=0)
        ).astype(BF16)

    gram_hh[...] = jnp.zeros_like(gram_hh)
    gram_hl[...] = jnp.zeros_like(gram_hl)

    def expand(k, high_ref, low_ref):
        source = source_recv[k]
        along_l, along_m = source[0:4], source[4:8]
        along_n = jnp.sqrt(1.0 - along_l * along_l - along_m * along_m)
        source = jnp.concatenate([along_l, along_m, along_n, jnp.zeros_like(along_n)], axis=0)
        first, second, third = three_parts(source)
        parts = jnp.concatenate([first, first, first, second, second, third], axis=0).astype(BF16)
        turns = dot(ant_parts[:, :96], parts)
        for lane in range(0, slots, LANES):
            piece = lane // LANES
            root = source_recv[k, 8 + piece : 9 + piece, :]
            for top in range(0, LANES, 64):
                cosine, sine = scaled_cos_sin(turns[lane + top : lane + top + 64], root)
                for base, value in ((0, cosine), (LANES, sine)):
                    high, low = split(value)
                    at = (pl.ds(base + top, 64), pl.ds(lane, LANES))
                    phased_hi[(k, *at)] = high
                    phased_lo[(k, *at)] = low
                    high_ref[at] = high
                    low_ref[at] = low

    def correlate(high_ref, low_ref):
        high = high_ref[...]
        gram_hh[...] += dot(high, high, NT)
        gram_hl[...] += dot(high, low_ref[...], NT)

    odd_hi[...] = jnp.zeros_like(odd_hi)
    odd_lo[...] = jnp.zeros_like(odd_lo)

    antenna_id = lax.broadcasted_iota(jnp.int32, (LANES, 512), 0)

    def build_one_hot(j, carry):
        at = pl.ds(pl.multiple_of(j * 512, 512), 512)
        left = (antenna_id == pairs_ref[0:1, at]).astype(F32).astype(BF16)
        left_twice[:LANES, at] = left
        left_twice[LANES:, at] = left
        one_right[:, at] = (antenna_id == pairs_ref[1:2, at]).astype(F32).astype(BF16)
        return carry

    lax.fori_loop(0, nb // 512, build_one_hot, 0)
    inputs[8].wait()

    @pl.when(q == centre)
    def _():
        piece = min(64, 2 * nch)

        def split_tables(j, carry):
            at = pl.ds(pl.multiple_of(j * piece, piece), piece)
            for i in range(2):
                tables_hi[i, at, :], tables_lo[i, at, :] = split(tables[i, at, :])
            return carry

        lax.fori_loop(0, 2 * nch // piece, split_tables, 0)

    @pl.when(q == centre)
    def _():
        pl.semaphore_wait(barrier, nch - 1)

    @pl.when(q != centre)
    def _():
        pl.semaphore_wait(barrier, 2 * (ns - 1) + nf - 1)


    def send_sources(step, carry):
        j = quad_at(s // 4, step, quads)
        for i in range(4):
            peer = j * 4 + i

            @pl.when(peer != s)
            def _():
                pltpu.make_async_remote_copy(
                    src_ref=source_send.at[peer], dst_ref=source_recv.at[s], send_sem=send1,
                    recv_sem=recv1.at[s // 4], device_id={"src": peer}, device_id_type=MESH,
                ).start()

        return carry

    lax.fori_loop(0, quads, send_sources, 0)

    @pl.when(q == centre)
    def _():
        dat_recv[q] = data_ref[...]

    @pl.when(q != centre)
    def _():
        pltpu.make_async_remote_copy(
            src_ref=data_ref, dst_ref=dat_recv.at[q], send_sem=send2, recv_sem=recv2.at[q],
            device_id={"freq": centre}, device_id_type=MESH,
        ).start()

    def forward(step, carry):
        j = quad_at(s // 4, step, quads)

        @pl.when(step == 0)
        def _():
            at = pl.ds(0, 3)
            pltpu.make_async_copy(source_send.at[at], source_recv.at[at], recv1.at[j]).wait()

        @pl.when(step != 0)
        def _():
            at = pl.ds(0, 4)
            pltpu.make_async_copy(source_send.at[at], source_recv.at[at], recv1.at[j]).wait()

        expand(j * 4, even_hi, even_lo)
        correlate(odd_hi, odd_lo)
        expand(j * 4 + 1, odd_hi, odd_lo)
        correlate(even_hi, even_lo)
        expand(j * 4 + 2, even_hi, even_lo)
        correlate(odd_hi, odd_lo)
        expand(j * 4 + 3, odd_hi, odd_lo)
        correlate(even_hi, even_lo)
        return carry

    lax.fori_loop(0, quads, forward, 0)
    correlate(odd_hi, odd_lo)

    gram = gram_hh[...] + 2.0 * gram_hl[...]
    even = gram[:LANES, :LANES] + gram[LANES:, LANES:]
    odd = gram[LANES:, :LANES] - gram[:LANES, LANES:]
    vis_re = 0.5 * (even + even.T)
    vis_im = 0.5 * (odd - odd.T)
    grid_hi, grid_lo = split(jnp.concatenate([vis_re, -vis_im], axis=0))
    grid_parts = jnp.concatenate([grid_hi, grid_lo], axis=1)

    pair = min(2, quads)

    def gather(step, carry):
        chosen = [quad_at(s // 4, quads - 1 - step * pair - i, quads) for i in range(pair)]
        rows = []
        for j in chosen:
            at = pl.ds(pl.multiple_of(j * 512, 512), 512)
            picked = dot(grid_parts, left_twice[:, at])
            right = one_right[:, at].astype(F32)
            rows.append([
                jnp.sum(picked[c * LANES : (c + 1) * LANES] * right, axis=0, keepdims=True) for c in range(2)
            ])
        for j, row in zip(chosen, rows):
            for i in range(4):
                for c in range(2):
                    vis_send[j * 4 + i, c : c + 1, :] = row[c][:, i * LANES : (i + 1) * LANES]
        for j in chosen:
            for i in range(4):
                peer = j * 4 + i

                @pl.when(jnp.logical_or(peer != s, q != centre))
                def _():
                    pltpu.make_async_remote_copy(
                        src_ref=vis_send.at[peer], dst_ref=vis_all.at[q * ns + s], send_sem=send3, recv_sem=recv3,
                        device_id={"src": peer, "freq": centre}, device_id_type=MESH,
                    ).start()

        return carry

    lax.fori_loop(0, quads // pair, gather, 0)

    def add_parts(k, carry):
        for top in range(0, 2 * LANES, 64):
            at = pl.ds(top, 64)
            phased_sum[k, at, :] = phased_hi[k, at, :].astype(F32) + 2.0 * phased_lo[k, at, :].astype(F32)
        return carry

    lax.fori_loop(0, ns, add_parts, 0)
    most = pl.ds(0, ns - 1)
    others = pl.ds(0, nf - 1)
    all_but_one = pl.ds(0, nch - 1)

    @pl.when(q == centre)
    def _():
        def take_data(step, carry):
            other = lax.rem(q + step, nf)
            pltpu.make_async_remote_copy(
                src_ref=data_ref, dst_ref=dat_recv.at[other], send_sem=send2, recv_sem=recv2.at[other],
                device_id={"freq": other}, device_id_type=MESH,
            ).wait_recv()
            return carry

        lax.fori_loop(1, nf, take_data, 0)

        def three_passes(i, high, low):
            both = dot(tables_hi[i], jnp.concatenate([high, low], axis=1))
            return both[:, :LANES] + both[:, LANES:] + dot(tables_lo[i], high)

        weight = jnp.transpose(jnp.broadcast_to(dw_ref[...], (LANES, nch)))
        spectra = [
            jnp.transpose(jnp.concatenate([dat_recv[i, c] for i in range(nf)], axis=0)) for c in range(2)
        ]
        vis_all[q * ns + s] = vis_send[s]
        pltpu.make_async_copy(vis_all.at[all_but_one], vis_all.at[all_but_one], recv3).wait()

        def pack(j, carry):
            at = pl.ds(pl.multiple_of(j * 16, 16), 16)
            vis_rows[at, :] = jnp.concatenate([vis_all[j * 8 + i] for i in range(8)], axis=0)
            return carry

        lax.fori_loop(0, nch // 8, pack, 0)
        vis_hi, vis_lo = split(vis_rows[...])
        spec = three_passes(0, vis_hi, vis_lo)
        spec_cot = jnp.concatenate(
            [weight * (spec[:nch] - spectra[0]), weight * (spec[nch:] - spectra[1])], axis=0
        )
        cot_hi, cot_lo = split(spec_cot)
        vis_rows[...] = three_passes(1, cot_hi, cot_lo)

        def send_cot(step, carry):
            j = quad_at(s // 4, quads - 1 - step, quads)
            for group in range(nf):
                first = group * ns + j * 4
                piece = vis_rows[pl.ds(pl.multiple_of(first * 2, 8), 8), :]
                for i in range(4):
                    peer = j * 4 + i
                    cot_all[first + i] = piece[2 * i : 2 * i + 2]

                    def send():
                        pltpu.make_async_remote_copy(
                            src_ref=cot_all.at[first + i], dst_ref=cot_recv.at[s], send_sem=send6,
                            recv_sem=recv6.at[s // 4], device_id={"src": peer, "freq": group},
                            device_id_type=MESH,
                        ).start()

                    if group == centre:
                        pl.when(peer != s)(send)
                    else:
                        send()
            return carry

        lax.fori_loop(0, quads, send_cot, 0)
        cot_recv[s] = cot_all[q * ns + s]

    many = min(4, quads)

    def scatter(half, carry):
        total = grids_ref[...]
        for i in range(many):
            step = half * many + i
            j = quad_at(s // 4, step, quads)
            with_own = jnp.logical_and(step == 0, q == centre)

            @pl.when(with_own)
            def _():
                pltpu.make_async_copy(cot_recv.at[pl.ds(0, 3)], cot_recv.at[pl.ds(0, 3)], recv6.at[j]).wait()

            @pl.when(jnp.logical_not(with_own))
            def _():
                pltpu.make_async_copy(cot_recv.at[pl.ds(0, 4)], cot_recv.at[pl.ds(0, 4)], recv6.at[j]).wait()

        for i in range(many):
            j = quad_at(s // 4, half * many + i, quads)
            at = pl.ds(pl.multiple_of(j * 512, 512), 512)
            right = one_right[:, at]
            parts = []
            for c in range(2):
                row = jnp.concatenate([cot_recv[j * 4 + i, c : c + 1, :] for i in range(4)], axis=1)
                parts.append(split(row))
            scaled = [right * parts[c][part] for part in range(2) for c in range(2)]
            total = total + dot(jnp.concatenate(scaled, axis=0), left_twice[:LANES, at], NT)
        grids_ref[...] = total
        return carry

    grids_ref[...] = jnp.zeros_like(grids_ref)
    lax.fori_loop(0, quads // many, scatter, 0)
    grids = grids_ref[...]
    grids = grids[: 2 * LANES] + grids[2 * LANES :]
    real, imag = grids[:LANES], grids[LANES:]
    real, imag = 0.5 * (real + real.T), 0.5 * (imag.T - imag)
    matrix = jnp.concatenate(
        [jnp.concatenate([real, -imag], axis=1), jnp.concatenate([imag, real], axis=1)], axis=0
    )
    matrix_parts = jnp.concatenate(split(matrix), axis=0)

    def pull_back(k):
        for lane in range(0, slots, 256):
            at = pl.ds(lane, 256)
            high = phased_hi[k, :, at]
            product = dot(matrix_parts, high)
            product = product[: 2 * LANES] + product[2 * LANES :]
            u_send[k, :, at] = jnp.sum(phased_sum[k, :, at] * product, axis=0, keepdims=True)

    def send_gradient(peer):
        pltpu.make_async_remote_copy(
            src_ref=u_send.at[peer], dst_ref=u_recv.at[s], send_sem=send7, recv_sem=recv7,
            device_id={"src": peer}, device_id_type=MESH,
        ).start()

    def backward(step, carry):
        j = quad_at(s // 4, quads - 1 - step, quads)
        for i in range(4):
            pull_back(j * 4 + i)
        for i in range(4):
            send_gradient(j * 4 + i)
        return carry

    lax.fori_loop(0, quads - 1, backward, 0)
    for step in (2, 1, 3):
        pull_back(in_quad(s, step))
    for step in (2, 1, 3):
        send_gradient(in_quad(s, step))
    pull_back(s)
    u_recv[s] = u_send[s]
    pltpu.make_async_copy(u_send.at[most], u_recv.at[most], recv7).wait()
    for i in range(ns):
        u_ref[i : i + 1, :] = u_recv[i]
    flux_send[0] = jnp.sum(u_ref[...], axis=0, keepdims=True)

    def send_flux(step, carry):
        other = lax.rem(q + step, nf)
        pltpu.make_async_remote_copy(
            src_ref=flux_send, dst_ref=flux_recv.at[pl.ds(q, 1)], send_sem=send8, recv_sem=recv8,
            device_id={"freq": other}, device_id_type=MESH,
        ).start()
        return carry

    lax.fori_loop(1, nf, send_flux, 0)
    flux_recv[q] = flux_send[0]
    pltpu.make_async_copy(source_send.at[most], source_recv.at[most], send1).wait()
    pltpu.make_async_copy(u_send.at[most], u_recv.at[most], send7).wait()

    @pl.when(q == centre)
    def _():
        pltpu.make_async_copy(vis_send.at[most], vis_send.at[most], send3).wait()
        pltpu.make_async_copy(cot_all.at[all_but_one], cot_all.at[all_but_one], send6).wait()

    @pl.when(q != centre)
    def _():
        pltpu.make_async_copy(vis_send, vis_send, send3).wait()
        pltpu.make_async_copy(data_ref, dat_recv.at[0], send2).wait()

    pltpu.make_async_copy(flux_recv.at[others], flux_recv.at[others], recv8).wait()
    total = flux_recv[0]
    for i in range(1, nf):
        total = total + flux_recv[i]
    total_ref[...] = total
    pltpu.make_async_copy(flux_recv.at[others], flux_recv.at[others], send8).wait()


def body(source_dirs, flux, beam, counts, antennas, pairs, data, delay_weight):
    ns, nf = lax.axis_size("src"), lax.axis_size("freq")
    slots = flux.shape[0]
    nch = ns * nf
    share = LANES // nf
    vmem, hbm = pl.BlockSpec(memory_space=pltpu.VMEM), pl.BlockSpec(memory_space=pltpu.HBM)
    dma = pltpu.SemaphoreType.DMA
    macs = 4 * ns * slots * 256 * 256
    tables = jnp.asarray(delay_tables(nch))
    inputs = (
        source_dirs, flux[None, :], beam, counts, antennas, pairs, jnp.transpose(data, (0, 2, 1)),
        delay_weight[None, :], tables,
    )
    gradient, total = pl.pallas_call(
        functools.partial(kernel, ns, nf, min(3, nf - 1)),
        out_shape=(
            pltpu.VMEM((ns, slots), F32),
            pltpu.VMEM((1, slots), F32),
        ),
        in_specs=[hbm] * len(inputs),
        out_specs=(vmem, vmem),
        scratch_shapes=[
            (pltpu.SMEM if i == 3 else pltpu.VMEM)(value.shape, value.dtype) for i, value in enumerate(inputs)
        ] + [
            pltpu.VMEM((ns, 12, LANES), F32),
            pltpu.VMEM((ns, 12, LANES), F32),
            pltpu.VMEM((ns, 2 * LANES, slots), BF16),
            pltpu.VMEM((ns, 2 * LANES, slots), BF16),
            pltpu.VMEM((ns, 2 * LANES, slots), F32),
            pltpu.VMEM((2 * LANES, ns * LANES), BF16),
            pltpu.VMEM((LANES, ns * LANES), BF16),
            pltpu.VMEM((4 * LANES, LANES), BF16),
            pltpu.VMEM((2 * LANES, slots), BF16),
            pltpu.VMEM((2 * LANES, slots), BF16),
            pltpu.VMEM((2 * LANES, slots), BF16),
            pltpu.VMEM((2 * LANES, slots), BF16),
            pltpu.VMEM((2 * LANES, 2 * LANES), F32),
            pltpu.VMEM((2 * LANES, 2 * LANES), F32),
            pltpu.VMEM((4 * LANES, LANES), F32),
            pltpu.VMEM((ns, 2, LANES), F32),
            pltpu.VMEM((nch, 2, LANES), F32),
            pltpu.VMEM((2 * nch, LANES), F32),
            pltpu.VMEM((nf, 2, share, nch), F32),
            pltpu.VMEM((2, 2 * nch, 2 * nch), BF16),
            pltpu.VMEM((2, 2 * nch, 2 * nch), BF16),
            pltpu.VMEM((nch, 2, LANES), F32),
            pltpu.VMEM((ns, 2, LANES), F32),
            pltpu.VMEM((ns, 1, slots), F32),
            pltpu.VMEM((ns, 1, slots), F32),
            pltpu.VMEM((1, 1, slots), F32),
            pltpu.VMEM((nf, 1, slots), F32),
            dma((len(inputs),)),
            dma, dma((ns // 4,)),
            dma, dma((nf,)),
            dma, dma,
            dma, dma((ns // 4,)),
            dma, dma,
            dma, dma,
        ],
        compiler_params=pltpu.CompilerParams(
            collective_id=0, has_side_effects=True, vmem_limit_bytes=63 * 1024 * 1024
        ),
        cost_estimate=pl.CostEstimate(flops=2 * macs, bytes_accessed=4 * 1024 * 1024, transcendentals=0),
    )(*inputs)
    return (total[0] / flux, 2.0 * gradient / beam)


def solution(mesh):
    in_specs = (
        P(None, "src"),
        P("src"),
        P("freq", "src"),
        P(),
        P(),
        P(),
        P(None, None, ("src", "freq")),
        P(),
    )
    out_specs = (P("src"), P("freq", "src"))
    return jax.shard_map(body, mesh=mesh, in_specs=in_specs, out_specs=out_specs, check_vma=False)
```
